256 devices in a mesh: row: 64 (over y, z, core), col: 4 (over x).
Axes of the slice: x: 4, y: 4, z: 8, core: 2. Of those that a mesh axis runs over, the one named last changes fastest.
Arguments:
- queries: bfloat16 [32768, 256], P(('row', 'col')), may hold values from -10 to 10, as said below
- candidates: bfloat16 [32768, 256], P(('row', 'col')), may hold values from -10 to 10, as said below
- block_mask: int32 [256, 256], replicated, may hold values 0 or 1
- row_class: int32 [32768], replicated, may hold values from 0 to 7
- col_class: int32 [32768], replicated, may hold values from 0 to 7
- cotangent: float32 [32768], P('row'), may hold values from -6 to 6
Outputs:
- query_grads: float32 [32768, 256], P(('row', 'col'))
- candidate_grads: float32 [32768, 256], P(('row', 'col'))
The draws below stay inside these ranges and needn't reach their ends.
Inputs may be any that keep to these rules, and one draw needn't show every extreme that they name: `queries`: one embedding a session. `candidates`: one embedding a session.
All inputs are finite; a program needn't handle non-finite values.
Results may differ from the reference program's by a relative error of at most 0.004.
Values may be sent and summed in bfloat16 or wider, within the bound.
A program may use at most 128 MiB of HBM per device.

```python
import math
import jax
import jax.numpy as jnp
from jax import lax

D = 256
BLOCK = 128
ROWS_DEV = 128
TOKENS = 32768
NB = 256
N_COL = 4


def column_factor(top):
    place = jnp.arange(TOKENS) // ROWS_DEV % N_COL
    return (1.0 + top * place.astype(jnp.float32) / max(N_COL - 1, 1))[:, None]


def draw_candidates(key, part):
    key = jax.random.fold_in(key, 1)
    values = jax.random.normal(key, (TOKENS, D), jnp.float32) * column_factor(0.9)
    return jnp.clip(values, -10.0, 10.0).astype(jnp.bfloat16)


def draw_queries(key, part):
    key = jax.random.fold_in(key, 2)
    values = jax.random.normal(key, (TOKENS, D), jnp.float32)
    return jnp.clip(values, -10.0, 10.0).astype(jnp.bfloat16)


def touch_ends(values, own_key, least, top_value):
    longest = values.shape.index(max(values.shape))
    spots = []
    for shift in (0, 1):
        where = [jax.random.randint(jax.random.fold_in(own_key, axis), (), 0, length) for axis, length in enumerate(values.shape)]
        where[longest] = (where[longest] + shift) % values.shape[longest]
        spots.append(tuple(where))
    return values.at[spots[0]].set(least).at[spots[1]].set(top_value)


def steps_of(key, shape, shards, smallest, high):
    loudness = 1.0
    for dim, blocks in shards:
        steps = jax.random.uniform(jax.random.fold_in(jax.random.fold_in(key, 6), dim), (blocks,), jnp.float32, smallest / len(shards), high / len(shards))
        loudness = loudness * jnp.repeat(jnp.exp(steps), shape[dim] // blocks).reshape((-1,) + (1,) * (len(shape) - 1 - dim))
    return loudness


def centred(stream_key, extent, scale, most, shards=(), kind=jnp.bfloat16):
    values = jax.random.normal(stream_key, extent, jnp.float32) * scale
    if len(shards) > 0:
        values = steps_of(stream_key, extent, shards, -0.22, 0.18) * values
    return jnp.clip(values, min=-most, max=most).astype(kind)


def setup_inputs(seed: int = 0) -> dict:
    streams_of = jax.random.split(jax.random.key(seed), 7)
    return {
        "queries": draw_queries(jax.random.fold_in(streams_of[6], 71), 0),
        "candidates": draw_candidates(jax.random.fold_in(streams_of[6], 71), 0),
        "block_mask": touch_ends((jax.random.randint(streams_of[2], (NB, NB), 0, 64) < 1).astype(jnp.int32), jax.random.fold_in(streams_of[2], 1), 0, 1),
        "row_class": touch_ends(jax.random.randint(streams_of[3], (TOKENS,), 0, 8), jax.random.fold_in(streams_of[3], 1), 0, 7).astype(jnp.int32),
        "col_class": touch_ends(jax.random.randint(streams_of[4], (TOKENS,), 0, 8), jax.random.fold_in(streams_of[4], 1), 0, 7).astype(jnp.int32),
        "cotangent": centred(streams_of[5], (TOKENS,), 1.0, 6.0, ((0, 64),), jnp.float32),
    }


def positive_table(col_ids, row_ids, block_mask, row_class, col_class):
    block_hits = jnp.take(jnp.take(block_mask.T, col_ids // BLOCK, axis=0), row_ids // BLOCK, axis=1)
    same_class = jnp.take(col_class, col_ids)[:, None] == jnp.take(row_class, row_ids)[None, :]
    return jnp.where((block_hits == 1) & same_class, 1.0, 0.0).astype(jnp.float32)

def reference(queries, candidates, block_mask, row_class, col_class, cotangent):
    scale = 1.0 / math.sqrt(D)
    span = math.gcd(TOKENS, 512)
    blocks = TOKENS // span
    all_ids = jnp.arange(TOKENS, dtype=jnp.int32)

    def one_block(total, index):
        start = (index * span).astype(jnp.int32)
        query_rows = lax.dynamic_slice_in_dim(queries, start, span, 0)
        weights = lax.dynamic_slice_in_dim(cotangent, start, span, 0)
        row_ids = start + jnp.arange(span, dtype=jnp.int32)
        scores = lax.dot_general(candidates, query_rows, (((1,), (1,)), ((), ())), preferred_element_type=jnp.float32) * scale
        hits = positive_table(all_ids, row_ids, block_mask, row_class, col_class)
        row_max = lax.optimization_barrier(jnp.max(scores, axis=0))
        row_lse = row_max + jnp.log(lax.optimization_barrier(jnp.sum(jnp.exp(scores - row_max), axis=0)))
        row_count = lax.optimization_barrier(jnp.sum(hits, axis=0))
        denom = jnp.maximum(row_count, 1.0)
        coef_soft = weights * row_count / denom
        coef_pos = weights / denom
        grads = (coef_soft * jnp.exp(scores - row_lse) - coef_pos * hits).astype(jnp.bfloat16)
        query_part = lax.dot_general(grads, candidates, (((0,), (0,)), ((), ())), preferred_element_type=jnp.float32) * scale
        total = total + jnp.dot(grads, query_rows, preferred_element_type=jnp.float32)
        return (total, query_part)
    total, parts = lax.scan(one_block, jnp.zeros((TOKENS, D), jnp.float32), jnp.arange(blocks, dtype=jnp.int32))
    return (parts.reshape(TOKENS, D), total * scale)
```

```python
import math

import jax
import jax.numpy as jnp
from jax import lax
from jax.experimental import pallas as pl
from jax.experimental.pallas import tpu as pltpu
from jax.sharding import PartitionSpec as P

MESH = pl.DeviceIdType.MESH
F32 = jnp.float32
BF16 = jnp.bfloat16
ROWS = 128
D = 256
NX, NY, NZ = 4, 4, 8
TILE = 2048
SLOTS = 16
CLASSES = 8
GROUP = 512
GROUPS = TILE // GROUP
NB = 256
LOG2E = math.log2(math.e)
NT = (((1,), (1,)), ((), ()))
TN = (((0,), (0,)), ((), ()))

OFFSETS = [(0, 0), (1, 0), (3, 0), (2, 0), (0, 1), (0, 3), (0, 2)]
OFFSETS += [(a, b) for a in (1, 3, 2) for b in (1, 3, 2)]
PLACE = {o: i for i, o in enumerate(OFFSETS)}


def split2(value):
    high = value.astype(BF16)
    return high, (value - high.astype(F32)).astype(BF16)


def as_row(value):
    return jnp.concatenate([value[s : s + 1, :] for s in range(SLOTS)], axis=1)


def kernel(
    q_own, c_own, mask_ref, rc_ref, cc_ref, cot_ref, dq_out, dc_out,
    qg, cg, qt, e, m_ref, l_ref, pt, pc, ot, post, st_own, st_sib, st_all, aqt,
    dqf, dcf, zs_sib, zr_sib, zp, zs1, zr1, zs2, zr2, xs1, xr1, xs2, xr2,
    q_ss, q_rs, qf_ss, qf_rs, c_ss, c_rs, t_ss, t_rs, zb_ss, zb_rs,
    z1_ss, z1_rs, z2_ss, z2_rs, x1_ss, x1_rs, x2_ss, x2_rs,
):
    scale = 1.0 / math.sqrt(D)
    kk = LOG2E * scale
    x = lax.axis_index("col")
    row = lax.axis_index("row")
    core = row % 2
    z = (row // 2) % NZ
    y = row // (2 * NZ)
    par = (x + y) % 2
    zpar = z % 2
    zsig = 1 - 2 * zpar

    def dev(dx, dy, dz, dcore):
        ny, nz, nc = (y + dy) % NY, (z + dz) % NZ, (core + dcore) % 2
        return ((ny * NZ + nz) * 2 + nc, (x + dx) % NX)

    sibling = dev(0, 0, 0, 1)
    pending = []

    def send(src, dst, ssem, rsem, to):
        copy = pltpu.make_async_remote_copy(
            src_ref=src, dst_ref=dst, send_sem=ssem, recv_sem=rsem, device_id=to, device_id_type=MESH
        )
        copy.start()
        pending.append(copy)
        return copy

    def arrived(dst, ssem, rsem):
        pltpu.make_async_remote_copy(
            src_ref=dst, dst_ref=dst, send_sem=ssem, recv_sem=rsem, device_id=sibling, device_id_type=MESH
        ).wait_recv()

    barrier = pltpu.get_barrier_semaphore()
    peers = [sibling]
    peers += [dev(d, 0, 0, 0) for d in (1, 2, 3)]
    peers += [dev(0, d, 0, 0) for d in (1, 2, 3)]
    peers += [dev(0, 0, d, 0) for d in (1, 2, 6, 7)]
    for peer in peers:
        pl.semaphore_signal(barrier, inc=1, device_id=peer, device_id_type=MESH)
    pl.semaphore_wait(barrier, len(peers))

    own_slot = 2 * z + core
    z_hops = (2, -2, 1, -1)
    for i, hop in enumerate(z_hops):
        send(q_own, qg.at[own_slot], q_ss.at[i], q_rs.at[i], dev(0, 0, hop, 0))
    for o in OFFSETS[1:7]:
        back = ((-o[0]) % NX, (-o[1]) % NY)
        send(c_own, cg.at[PLACE[back]], c_ss.at[PLACE[back]], c_rs.at[PLACE[back]], dev(o[0], o[1], 0, 0))
    send(q_own, qg.at[own_slot], qf_ss.at[7], qf_rs.at[7], sibling)
    qg[own_slot] = q_own[...]
    cg[0] = c_own[...]

    lane256 = lax.broadcasted_iota(jnp.int32, (SLOTS, NB), 1)
    slot256 = lax.broadcasted_iota(jnp.int32, (SLOTS, NB), 0)
    sel_q = jnp.where(lane256 == (y * SLOTS + slot256) * NX + x, 1.0, 0.0).astype(BF16)
    c_block = jnp.zeros((SLOTS, NB), jnp.int32)
    for b, (dx, dy) in enumerate(OFFSETS):
        block = ((((y + dy) % NY) * NZ + z) * 2 + core) * NX + (x + dx) % NX
        c_block = jnp.where(slot256 == b, block, c_block)
    sel_c = jnp.where(lane256 == c_block, 1.0, 0.0).astype(BF16)
    mask = mask_ref[...].astype(F32).astype(BF16)
    rc_all = rc_ref[...].astype(F32).astype(BF16)
    cc_all = cc_ref[...].astype(F32)
    m_sel = jnp.dot(sel_q, mask, preferred_element_type=F32).astype(BF16)
    rc = jnp.dot(sel_q, rc_all, preferred_element_type=F32)
    cc = jnp.dot(sel_c, cc_all.astype(BF16), preferred_element_type=F32)
    lane128 = lax.broadcasted_iota(jnp.int32, (ROWS, ROWS), 1)
    hist = jnp.zeros((NB, ROWS), F32)
    for k in range(CLASSES):
        column = jnp.where(lane128 == k, 1.0, 0.0).astype(BF16)
        same = jnp.where(cc_all == float(k), 1.0, 0.0).astype(BF16)
        hist = hist + jnp.dot(same, column, preferred_element_type=F32)
    per_class = jnp.dot(m_sel, hist.astype(BF16), preferred_element_type=F32)
    count = jnp.zeros((SLOTS, ROWS), F32)
    for k in range(CLASSES):
        count = jnp.where(rc == float(k), per_class[:, k : k + 1], count)
    denom = jnp.maximum(count, 1.0)
    class_of = (lax.broadcasted_iota(jnp.int32, (ROWS, ROWS), 0) % CLASSES).astype(F32)
    slot_of = lax.broadcasted_iota(jnp.int32, (ROWS, ROWS), 0) // CLASSES

    def repeated(value):
        return jnp.broadcast_to(value[:, None, :], (SLOTS, CLASSES, NB)).reshape(ROWS, NB)

    sel_c_rows = repeated(sel_c.astype(F32)).astype(BF16)
    m_sel_rows = repeated(m_sel.astype(F32)).astype(BF16)
    hit_q = lax.dot_general(sel_c_rows, m_sel, NT, preferred_element_type=F32)
    hit_c = lax.dot_general(m_sel_rows, sel_c, NT, preferred_element_type=F32)
    for s in range(SLOTS):
        lanes = slice(s * ROWS, (s + 1) * ROWS)
        picked = jnp.where(rc[s : s + 1, :] == class_of, hit_q[:, s : s + 1], 0.0).astype(BF16)
        pt[0:ROWS, lanes] = picked
        pt[ROWS:NB, lanes] = picked
        picked = jnp.where(cc[s : s + 1, :] == class_of, hit_c[:, s : s + 1], 0.0).T.astype(BF16)
        pc[lanes, 0:ROWS] = picked
        pc[lanes, ROWS:NB] = picked

    def c_slot(even, odd):
        return even + par * (odd - even)

    turn = [
        (c_slot(4, 1), 1 - par, par, [((d, 0), (0, d)) for d in (1, 3, 2)], ((0, 1), (1, 0))),
        (c_slot(5, 2), 1 - par, par, [((d, 0), (0, d)) for d in (1, 3, 2)], ((0, 3), (3, 0))),
        (c_slot(3, 6), par, 1 - par, [((0, d), (d, 0)) for d in (1, 3, 2)], ((2, 0), (0, 2))),
    ]
    sent = 0
    for slot, fx, fy, hops, origin in turn:
        arrived(cg.at[slot], c_ss.at[slot], c_rs.at[slot])
        for even, odd in hops:
            d = max(even)
            there = [
                PLACE[((o[0] - h[0]) % NX, (o[1] - h[1]) % NY)] for o, h in zip(origin, (even, odd))
            ]
            there = c_slot(*there)
            send(cg.at[slot], cg.at[there], c_ss.at[7 + sent], c_rs.at[there], dev(fx * d, fy * d, 0, 0))
            sent += 1

    def q_slot(dz):
        return 2 * ((z + dz) % NZ) + core

    def pass_on(i, dz):
        slot = q_slot(dz)
        send(qg.at[slot], qg.at[slot], qf_ss.at[i], qf_rs.at[i], sibling)

    for i in (0, 1):
        slot = q_slot(-z_hops[i])
        arrived(qg.at[slot], q_ss.at[i], q_rs.at[i])
    far = q_slot(-2 * zsig)
    send(qg.at[far], qg.at[far], q_ss.at[4], q_rs.at[4], dev(0, 0, 2 * zsig, 0))
    slot = q_slot(-2)
    send(qg.at[slot], qg.at[slot], q_ss.at[5], q_rs.at[5], dev(0, 0, 1, 0))
    slot = q_slot(2)
    send(qg.at[slot], qg.at[slot], q_ss.at[6], q_rs.at[6], dev(0, 0, -1, 0))
    pass_on(0, -2)
    pass_on(1, 2)
    for i in (2, 3):
        slot = q_slot(-z_hops[i])
        arrived(qg.at[slot], q_ss.at[i], q_rs.at[i])
        pass_on(i, -z_hops[i])
    for i, dz in ((4, 4), (5, -3), (6, 3)):
        slot = q_slot(dz)
        arrived(qg.at[slot], q_ss.at[i], q_rs.at[i])
        pass_on(i, dz)
    for i, dz in ((7, 0), (0, -2), (1, 2), (2, -1), (3, 1), (4, 4), (5, -3), (6, 3)):
        slot = 2 * ((z + dz) % NZ) + 1 - core
        arrived(qg.at[slot], qf_ss.at[i], qf_rs.at[i])
    for slot in (c_slot(1, 4), c_slot(2, 5), c_slot(6, 3)):
        arrived(cg.at[slot], c_ss.at[slot], c_rs.at[slot])

    q_all = qg[...].reshape(TILE, D)
    for g in range(GROUPS):
        first = g * GROUP // ROWS
        for slot in range(max(first, 7), first + GROUP // ROWS):
            arrived(cg.at[slot], c_ss.at[slot], c_rs.at[slot])
        rows = slice(g * GROUP, (g + 1) * GROUP)
        c_rows = cg[first : first + GROUP // ROWS].reshape(GROUP, D)
        scores = lax.dot_general(c_rows, q_all, NT, preferred_element_type=F32)
        top = jnp.max(scores, axis=0, keepdims=True)
        grown = jnp.exp2((scores - top) * kk)
        m_ref[g : g + 1, :] = top
        l_ref[g : g + 1, :] = jnp.sum(grown, axis=0, keepdims=True)
        e[rows, :] = grown.astype(BF16)
    m_groups = m_ref[0:GROUPS, :]
    m_tile = jnp.max(m_groups, axis=0, keepdims=True)
    shrink = jnp.exp2((m_groups - m_tile) * kk)
    l_tile = jnp.sum(l_ref[0:GROUPS, :] * shrink, axis=0, keepdims=True)

    for s in range(SLOTS):
        lanes = slice(s * ROWS, (s + 1) * ROWS)
        st_own[s : s + 1, :] = m_tile[:, lanes]
        st_own[SLOTS + s : SLOTS + s + 1, :] = l_tile[:, lanes]
    st_own[32:40, :] = jnp.broadcast_to(cot_ref[pl.ds(x, 1), :], (8, ROWS))
    send(st_own, st_sib, t_ss.at[0], t_rs.at[0], sibling)
    for s in range(SLOTS):
        lanes = slice(s * ROWS, (s + 1) * ROWS)
        qt[:, lanes] = qg[s].T
    arrived(st_sib, t_ss.at[0], t_rs.at[0])
    m_a, m_b = st_own[0:SLOTS, :], st_sib[0:SLOTS, :]
    m_pair = jnp.maximum(m_a, m_b)
    l_pair = st_own[SLOTS:32, :] * jnp.exp2((m_a - m_pair) * kk)
    l_pair = l_pair + st_sib[SLOTS:32, :] * jnp.exp2((m_b - m_pair) * kk)
    cot_a, cot_b = st_own[32:40, :], st_sib[32:40, :]
    here = lax.broadcasted_iota(jnp.int32, (8, ROWS), 0) == core
    st_all[z, 0:SLOTS, :] = m_pair
    st_all[z, SLOTS:32, :] = l_pair
    st_all[z, 32:40, :] = jnp.where(here, cot_a, cot_b)
    for d in range(1, NZ):
        send(st_all.at[z], st_all.at[z], t_ss.at[d], t_rs.at[d], dev(0, 0, d, 0))

    for g in range(GROUPS):
        first = g * GROUP // ROWS
        rows = slice(g * GROUP, (g + 1) * GROUP)
        c_rows = cg[first : first + GROUP // ROWS].reshape(GROUP, D)
        part = lax.dot_general(c_rows, e[rows, :], TN, preferred_element_type=F32) * shrink[g : g + 1, :]
        if g == 0:
            ot[...] = part
        else:
            ot[...] += part
    own_class = [
        jnp.where((cc[b : b + 1, :] == class_of) & (slot_of == b), 1.0, 0.0).astype(BF16) for b in range(SLOTS)
    ]
    sums = jnp.dot(
        jnp.concatenate(own_class, axis=1), cg[...].reshape(TILE, D), preferred_element_type=F32
    )
    sums = jnp.concatenate(split2(sums), axis=0)
    post[...] = lax.dot_general(sums, pt[...], TN, preferred_element_type=F32)

    for d in range(1, NZ):
        slot = (z - d + NZ) % NZ
        arrived(st_all.at[slot], t_ss.at[d], t_rs.at[d])
    m_all = st_all[0, 0:SLOTS, :]
    for s in range(1, NZ):
        m_all = jnp.maximum(m_all, st_all[s, 0:SLOTS, :])
    l_all = jnp.zeros((SLOTS, ROWS), F32)
    for s in range(NZ):
        l_all = l_all + st_all[s, SLOTS:32, :] * jnp.exp2((st_all[s, 0:SLOTS, :] - m_all) * kk)
    cot = jnp.concatenate([st_all[s, 32:34, :] for s in range(NZ)], axis=0)
    coef_pos = cot / denom
    soft = cot * count / denom / l_all
    soft_row, top_row, pos_row = as_row(soft), as_row(m_all), as_row(coef_pos)
    a_groups = soft_row * jnp.exp2((m_groups - top_row) * kk)
    a_tile = soft_row * jnp.exp2((m_tile - top_row) * kk)

    def dq_tile(slot):
        lanes = pl.ds(pl.multiple_of(slot * ROWS, ROWS), ROWS)
        return lanes

    dq_all = ot[...] * a_tile - post[...] * pos_row
    for s in range(SLOTS):
        dqf[s] = dq_all[:, s * ROWS : (s + 1) * ROWS]
    for s in range(NZ):
        zs_sib[s] = dqf[2 * s + 1 - core].astype(BF16)
    send(zs_sib, zr_sib, zb_ss.at[0], zb_rs.at[0], sibling)

    weights = [
        jnp.where((rc[s : s + 1, :] == class_of) & (slot_of == s), -coef_pos[s : s + 1, :], 0.0)
        for s in range(SLOTS)
    ]
    weights = jnp.concatenate(split2(jnp.concatenate(weights, axis=1)), axis=0)
    sums_q = jnp.dot(weights, q_all, preferred_element_type=F32)
    sums_q = sums_q[0:ROWS, :] + sums_q[ROWS:NB, :]
    sums_q = jnp.concatenate(split2(sums_q), axis=0)

    def dc_group(g):
        first = g * GROUP // ROWS
        rows = slice(g * GROUP, (g + 1) * GROUP)
        aqt[...] = (qt[...].astype(F32) * a_groups[g : g + 1, :]).astype(BF16)
        part = lax.dot_general(e[rows, :], aqt[...], NT, preferred_element_type=F32)
        part = part + jnp.dot(pc[rows, :], sums_q, preferred_element_type=F32)
        dcf[first : first + GROUP // ROWS] = part.reshape(GROUP // ROWS, ROWS, D)

    hub = {2: 0, 1: 1, 3: 2}

    def dc_send(slot):
        a, b = OFFSETS[slot]
        i = slot - 7
        odd = (par + a + b) % 2
        xs1[i] = dcf[slot].astype(BF16)
        even_to = hub[a] * 3 + (-b) % NY - 1
        odd_to = hub[b] * 3 + (-a) % NX - 1
        there = even_to + odd * (odd_to - even_to)
        send(xs1.at[i], xr1.at[there], x1_ss.at[i], x1_rs.at[there], dev(odd * a, (1 - odd) * b, 0, 0))

    dc_group(3)
    for slot in (12, 13, 14, 15):
        dc_send(slot)

    arrived(zr_sib, zb_ss.at[0], zb_rs.at[0])
    for s in range(NZ):
        zp[s] = dqf[2 * s + core] + zr_sib[s].astype(F32)
    for i, (target, hop) in enumerate(((-3, -1), (3, 1), (4, -2 * zsig))):
        zs1[i] = zp[(z + target + NZ) % NZ].astype(BF16)
        send(zs1.at[i], zr1.at[i], z1_ss.at[i], z1_rs.at[i], dev(0, 0, hop, 0))
    for i, target in ((2, -1), (3, 1)):
        zs2[i] = zp[(z + target + NZ) % NZ].astype(BF16)
        send(zs2.at[i], zr2.at[i], z2_ss.at[i], z2_rs.at[i], dev(0, 0, target, 0))

    dc_group(2)
    for slot in (8, 9, 10, 11):
        dc_send(slot)
    dc_group(1)
    dc_send(7)
    dc_group(0)
    for i, (slot, there, even, odd) in enumerate(
        (
            (c_slot(6, 3), c_slot(6, 3), (0, 2), (2, 0)),
            (c_slot(1, 4), c_slot(2, 5), (1, 0), (0, 1)),
            (c_slot(2, 5), c_slot(1, 4), (3, 0), (0, 3)),
        )
    ):
        xs2[i] = dcf[slot].astype(BF16)
        to = dev(even[0] + par * (odd[0] - even[0]), even[1] + par * (odd[1] - even[1]), 0, 0)
        send(xs2.at[i], xr2.at[there - 1], x2_ss.at[i], x2_rs.at[there - 1], to)

    for i in range(3):
        arrived(zr1.at[i], z1_ss.at[i], z1_rs.at[i])
    far = zr1[2].astype(F32)
    down = zp[(z + NZ - 2) % NZ] + zr1[0].astype(F32) + jnp.where(zpar == 0, far, 0.0)
    up = zp[(z + 2) % NZ] + zr1[1].astype(F32) + jnp.where(zpar == 1, far, 0.0)
    zs2[0] = down.astype(BF16)
    zs2[1] = up.astype(BF16)
    send(zs2.at[0], zr2.at[0], z2_ss.at[0], z2_rs.at[0], dev(0, 0, -2, 0))
    send(zs2.at[1], zr2.at[1], z2_ss.at[1], z2_rs.at[1], dev(0, 0, 2, 0))

    for j, (slot, there, even, odd) in enumerate(
        (
            (c_slot(3, 6), c_slot(3, 6), (2, 0), (0, 2)),
            (c_slot(4, 1), c_slot(5, 2), (0, 1), (1, 0)),
            (c_slot(5, 2), c_slot(4, 1), (0, 3), (3, 0)),
        )
    ):
        total = dcf[slot]
        for d in range(3):
            arrived(xr1.at[3 * j + d], x1_ss.at[3 * j + d], x1_rs.at[3 * j + d])
            total = total + xr1[3 * j + d].astype(F32)
        xs2[3 + j] = total.astype(BF16)
        to = dev(even[0] + par * (odd[0] - even[0]), even[1] + par * (odd[1] - even[1]), 0, 0)
        send(xs2.at[3 + j], xr2.at[there - 1], x2_ss.at[3 + j], x2_rs.at[there - 1], to)

    total = zp[z]
    for i in (2, 3, 0, 1):
        arrived(zr2.at[i], z2_ss.at[i], z2_rs.at[i])
        total = total + zr2[i].astype(F32)
    dq_out[...] = total.T * scale
    total = dcf[0]
    for i in range(6):
        arrived(xr2.at[i], x2_ss.at[i], x2_rs.at[i])
        total = total + xr2[i].astype(F32)
    dc_out[...] = total * scale
    for copy in pending:
        copy.wait_send()


def shards(queries, candidates, block_mask, row_class, col_class, cotangent):
    dma = pltpu.SemaphoreType.DMA
    vmem = pltpu.VMEM
    block = (D, ROWS)
    scratch = [
        vmem((SLOTS, ROWS, D), BF16),
        vmem((SLOTS, ROWS, D), BF16),
        vmem((D, TILE), BF16),
        vmem((TILE, TILE), BF16),
        vmem((8, TILE), F32),
        vmem((8, TILE), F32),
        vmem((NB, TILE), BF16),
        vmem((TILE, NB), BF16),
        vmem((D, TILE), F32),
        vmem((D, TILE), F32),
        vmem((40, ROWS), F32),
        vmem((40, ROWS), F32),
        vmem((NZ, 40, ROWS), F32),
        vmem((D, TILE), BF16),
        vmem((SLOTS,) + block, F32),
        vmem((SLOTS, ROWS, D), F32),
        vmem((NZ,) + block, BF16),
        vmem((NZ,) + block, BF16),
        vmem((NZ,) + block, F32),
        vmem((3,) + block, BF16),
        vmem((3,) + block, BF16),
        vmem((4,) + block, BF16),
        vmem((4,) + block, BF16),
        vmem((9, ROWS, D), BF16),
        vmem((9, ROWS, D), BF16),
        vmem((6, ROWS, D), BF16),
        vmem((6, ROWS, D), BF16),
        dma((7,)), dma((7,)), dma((8,)), dma((8,)), dma((16,)), dma((16,)), dma((8,)), dma((8,)),
        dma((1,)), dma((1,)), dma((3,)), dma((3,)), dma((4,)), dma((4,)),
        dma((9,)), dma((9,)), dma((6,)), dma((6,)),
    ]
    out = jax.ShapeDtypeStruct((ROWS, D), F32)
    return pl.pallas_call(
        kernel,
        out_shape=(out, out),
        in_specs=[pl.BlockSpec(memory_space=vmem)] * 6,
        out_specs=(pl.BlockSpec(memory_space=vmem), pl.BlockSpec(memory_space=vmem)),
        scratch_shapes=scratch,
        compiler_params=pltpu.CompilerParams(
            collective_id=0, has_side_effects=True, vmem_limit_bytes=56 * 2**20
        ),
    )(
        queries,
        candidates,
        block_mask,
        row_class.reshape(NB, ROWS),
        col_class.reshape(NB, ROWS),
        cotangent.reshape(NX, ROWS),
    )


def solution(mesh):
    in_specs = (P(("row", "col"), None), P(("row", "col"), None), P(), P(), P(), P("row"))
    out_specs = (P(("row", "col"), None), P(("row", "col"), None))
    return jax.shard_map(shards, mesh=mesh, in_specs=in_specs, out_specs=out_specs, check_vma=False)
```

```python
import math

import jax
import jax.numpy as jnp
from jax import lax
from jax.experimental import pallas as pl
from jax.experimental.pallas import tpu as pltpu
from jax.sharding import PartitionSpec as P

MESH = pl.DeviceIdType.MESH
F32 = jnp.float32
BF16 = jnp.bfloat16
ROWS = 128
D = 256
NX, NY, NZ = 4, 4, 8
TILE = 2048
SLOTS = 16
CLASSES = 8
NB = 256
LOG2E = math.log2(math.e)
NT = (((1,), (1,)), ((), ()))
TN = (((0,), (0,)), ((), ()))

OFFSETS = [(0, 0), (1, 0), (3, 0), (2, 0), (0, 1), (0, 3), (0, 2)]
OFFSETS += [(1, 1), (1, 3), (3, 1), (3, 3), (1, 2), (3, 2), (2, 1), (2, 3), (2, 2)]
PLACE = {o: i for i, o in enumerate(OFFSETS)}
GROUPS = ((0, 7), (7, 10), (10, 13), (13, 16))
Q_OFFSETS = [(0, 0), (-2, 0), (2, 0), (-1, 0), (0, 1), (-2, 1), (2, 1), (-1, 1)]
Q_OFFSETS += [(1, 0), (4, 0), (-3, 0), (3, 0), (1, 1), (4, 1), (-3, 1), (3, 1)]
Q_PLACE = {o: i for i, o in enumerate(Q_OFFSETS)}
OWN_CORE = (0, 1, 2, 3, 8, 9, 10, 11)


def split2(value):
    high = value.astype(BF16)
    return high, (value - high.astype(F32)).astype(BF16)


def as_row(rows):
    return jnp.concatenate(rows, axis=1)


def lanes_of(slot):
    return slice(slot * ROWS, (slot + 1) * ROWS)


def kernel(
    q_own, c_own, mask_hbm, rc_hbm, cc_hbm, cot_hbm, dq_out, dc_out,
    mask_ref, rc_ref, cc_ref, cot_ref, aux,
    qg, cg, qt, e, m_ref, l_ref, pt, pc, ot, post, st_own, st_sib, st_all, st_end, aqt,
    dcf, zs_sib, zr_sib, zp, zs1, zr1, zs2, zr2, xs1, xr1, xs2, xr2,
    in_s, q_ss, q_rs, qf_ss, qf_rs, a_ss, a_rs, af_ss, af_rs, c_ss, c_rs, t_ss, t_rs, zb_ss, zb_rs,
    z1_ss, z1_rs, z2_ss, z2_rs, x1_ss, x1_rs, x2_ss, x2_rs,
):
    kk = LOG2E / math.sqrt(D)
    x = lax.axis_index("col")
    row = lax.axis_index("row")
    core = row % 2
    z = (row // 2) % NZ
    y = row // (2 * NZ)
    par = (x + y) % 2
    zpar = z % 2
    zsig = 1 - 2 * zpar

    def dev(dx, dy, dz, dcore):
        ny, nz, nc = (y + dy) % NY, (z + dz) % NZ, (core + dcore) % 2
        return ((ny * NZ + nz) * 2 + nc, (x + dx) % NX)

    sibling = dev(0, 0, 0, 1)
    pending = []

    def send(src, dst, ssem, rsem, to):
        copy = pltpu.make_async_remote_copy(
            src_ref=src, dst_ref=dst, send_sem=ssem, recv_sem=rsem, device_id=to, device_id_type=MESH
        )
        copy.start()
        pending.append(copy)

    def arrived(dst, ssem, rsem):
        pltpu.make_async_remote_copy(
            src_ref=dst, dst_ref=dst, send_sem=ssem, recv_sem=rsem, device_id=sibling, device_id_type=MESH
        ).wait_recv()

    barrier = pltpu.get_barrier_semaphore()
    peers = [dev(0, 0, d, 0) for d in (2, 6, 1, 7)]
    peers += [dev(d, 0, 0, 0) for d in (2, 1, 3)]
    peers += [dev(0, d, 0, 0) for d in (2, 1, 3)]
    peers += [sibling]
    for peer in peers:
        pl.semaphore_signal(barrier, inc=1, device_id=peer, device_id_type=MESH)
    loads = [
        pltpu.make_async_copy(src, dst, in_s.at[i])
        for i, (src, dst) in enumerate(
            (
                (cot_hbm, cot_ref), (mask_hbm, mask_ref), (rc_hbm, rc_ref), (cc_hbm, cc_ref),
                (q_own, qg.at[0]), (c_own, cg.at[0]),
            )
        )
    ]
    for load in loads:
        load.start()
    pl.semaphore_wait(barrier, len(peers))

    z_hops = (2, -2, 1, -1)
    for i, hop in enumerate(z_hops):
        send(q_own, qg.at[Q_PLACE[-hop, 0]], q_ss.at[i], q_rs.at[i], dev(0, 0, hop, 0))
    for o in OFFSETS[1:7]:
        back = PLACE[(-o[0]) % NX, (-o[1]) % NY]
        send(c_own, cg.at[back], c_ss.at[back], c_rs.at[back], dev(o[0], o[1], 0, 0))
    send(q_own, qg.at[Q_PLACE[0, 1]], qf_ss.at[7], qf_rs.at[7], sibling)
    for load in loads:
        load.wait()
    aux[0] = jnp.broadcast_to(cot_ref[pl.ds(x, 1), :], (8, ROWS))
    for i, hop in enumerate(z_hops):
        send(aux.at[0], aux.at[Q_PLACE[-hop, 0]], a_ss.at[i], a_rs.at[i], dev(0, 0, hop, 0))
    send(aux.at[0], aux.at[Q_PLACE[0, 1]], af_ss.at[7], af_rs.at[7], sibling)

    lane256 = lax.broadcasted_iota(jnp.int32, (SLOTS, NB), 1)
    slot256 = lax.broadcasted_iota(jnp.int32, (SLOTS, NB), 0)
    q_block = jnp.zeros((SLOTS, NB), jnp.int32)
    for s, (dz, dc) in enumerate(Q_OFFSETS):
        block = ((y * NZ + (z + dz) % NZ) * 2 + (core + dc) % 2) * NX + x
        q_block = jnp.where(slot256 == s, block, q_block)
    sel_q = jnp.where(lane256 == q_block, 1.0, 0.0).astype(BF16)
    c_block = jnp.zeros((SLOTS, NB), jnp.int32)
    for b, (dx, dy) in enumerate(OFFSETS):
        block = ((((y + dy) % NY) * NZ + z) * 2 + core) * NX + (x + dx) % NX
        c_block = jnp.where(slot256 == b, block, c_block)
    sel_c = jnp.where(lane256 == c_block, 1.0, 0.0).astype(BF16)
    mask = mask_ref[...].astype(F32).astype(BF16)
    rc_all = rc_ref[...].astype(F32).astype(BF16)
    cc_all = cc_ref[...].astype(F32)
    m_sel = jnp.dot(sel_q, mask, preferred_element_type=F32).astype(BF16)
    rc = jnp.dot(sel_q, rc_all, preferred_element_type=F32)
    cc = jnp.dot(sel_c, cc_all.astype(BF16), preferred_element_type=F32)
    lane128 = lax.broadcasted_iota(jnp.int32, (ROWS, ROWS), 1)
    hist = jnp.zeros((NB, ROWS), F32)
    for k in range(CLASSES):
        column = jnp.where(lane128 == k, 1.0, 0.0).astype(BF16)
        same = jnp.where(cc_all == float(k), 1.0, 0.0).astype(BF16)
        hist = hist + jnp.dot(same, column, preferred_element_type=F32)
    per_class = jnp.dot(m_sel, hist.astype(BF16), preferred_element_type=F32)
    count = jnp.zeros((SLOTS, ROWS), F32)
    for k in range(CLASSES):
        count = jnp.where(rc == float(k), per_class[:, k : k + 1], count)
    per_count = 1.0 / jnp.maximum(count, 1.0)
    class_of = (lax.broadcasted_iota(jnp.int32, (ROWS, ROWS), 0) % CLASSES).astype(F32)
    slot_of = lax.broadcasted_iota(jnp.int32, (ROWS, ROWS), 0) // CLASSES

    def repeated(value):
        return jnp.broadcast_to(value[:, None, :], (SLOTS, CLASSES, NB)).reshape(ROWS, NB)

    sel_c_rows = repeated(sel_c.astype(F32)).astype(BF16)
    m_sel_rows = repeated(m_sel.astype(F32)).astype(BF16)
    hit_q = lax.dot_general(sel_c_rows, m_sel, NT, preferred_element_type=F32)
    hit_c = lax.dot_general(m_sel_rows, sel_c, NT, preferred_element_type=F32)
    for s in range(SLOTS):
        picked = jnp.where(rc[s : s + 1, :] == class_of, hit_q[:, s : s + 1], 0.0).astype(BF16)
        pt[0:ROWS, lanes_of(s)] = picked
        pt[ROWS:NB, lanes_of(s)] = picked
        picked = jnp.where(cc[s : s + 1, :] == class_of, hit_c[:, s : s + 1], 0.0).T.astype(BF16)
        pc[lanes_of(s), 0:ROWS] = picked
        pc[lanes_of(s), ROWS:NB] = picked

    def c_slot(even, odd):
        return even + par * (odd - even)

    turn = [
        (c_slot(4, 1), 1 - par, par, [((d, 0), (0, d)) for d in (1, 3, 2)], ((0, 1), (1, 0))),
        (c_slot(5, 2), 1 - par, par, [((d, 0), (0, d)) for d in (1, 3, 2)], ((0, 3), (3, 0))),
        (c_slot(3, 6), par, 1 - par, [((0, d), (d, 0)) for d in (1, 3, 2)], ((2, 0), (0, 2))),
    ]
    forwards = [0]

    def c_forward(slot, fx, fy, hops, origin):
        arrived(cg.at[slot], c_ss.at[slot], c_rs.at[slot])
        for even, odd in hops:
            d = max(even)
            there = [
                PLACE[((o[0] - h[0]) % NX, (o[1] - h[1]) % NY)] for o, h in zip(origin, (even, odd))
            ]
            there = c_slot(*there)
            i = 7 + forwards[0]
            send(cg.at[slot], cg.at[there], c_ss.at[i], c_rs.at[there], dev(fx * d, fy * d, 0, 0))
            forwards[0] += 1

    def q_arrived(i, dz):
        slot = Q_PLACE[dz, 0]
        arrived(qg.at[slot], q_ss.at[i], q_rs.at[i])

    def q_pass(i, dz):
        here, there = Q_PLACE[dz, 0], Q_PLACE[dz, 1]
        send(qg.at[here], qg.at[there], qf_ss.at[i], qf_rs.at[i], sibling)

    def a_pass(i, dz):
        here, there = Q_PLACE[dz, 0], Q_PLACE[dz, 1]
        arrived(aux.at[here], a_ss.at[i], a_rs.at[i])
        send(aux.at[here], aux.at[there], af_ss.at[i], af_rs.at[i], sibling)

    def onward(ref, ss, rs):
        far = Q_PLACE[-2, 0] + zpar * (Q_PLACE[2, 0] - Q_PLACE[-2, 0])
        send(ref.at[far], ref.at[Q_PLACE[4, 0]], ss.at[4], rs.at[4], dev(0, 0, 2 * zsig, 0))
        send(ref.at[Q_PLACE[-2, 0]], ref.at[Q_PLACE[-3, 0]], ss.at[5], rs.at[5], dev(0, 0, 1, 0))
        send(ref.at[Q_PLACE[2, 0]], ref.at[Q_PLACE[3, 0]], ss.at[6], rs.at[6], dev(0, 0, -1, 0))

    c_forward(*turn[0])
    c_forward(*turn[1])
    q_arrived(0, -2)
    q_arrived(1, 2)
    onward(qg, q_ss, q_rs)
    c_forward(*turn[2])
    q_pass(0, -2)
    q_pass(1, 2)
    q_arrived(2, -1)
    q_pass(2, -1)
    q_arrived(3, 1)
    q_pass(3, 1)
    a_pass(0, -2)
    a_pass(1, 2)
    a_pass(2, -1)
    a_pass(3, 1)
    onward(aux, a_ss, a_rs)
    for slot in (c_slot(1, 4), c_slot(2, 5), c_slot(6, 3)):
        arrived(cg.at[slot], c_ss.at[slot], c_rs.at[slot])

    def wave(g, q_first, q_last):
        first, last = GROUPS[g]
        rows = slice(first * ROWS, last * ROWS)
        lanes = slice(q_first * ROWS, q_last * ROWS)
        c_rows = cg[first:last].reshape((last - first) * ROWS, D)
        q_rows = qg[q_first:q_last].reshape((q_last - q_first) * ROWS, D)
        scores = lax.dot_general(c_rows, q_rows, NT, preferred_element_type=F32)
        top = jnp.max(scores, axis=0, keepdims=True)
        grown = jnp.exp2((scores - top) * kk)
        m_ref[g : g + 1, lanes] = top
        l_ref[g : g + 1, lanes] = jnp.sum(grown, axis=0, keepdims=True)
        e[rows, lanes] = grown.astype(BF16)

    wave(0, 0, 4)
    for i, dz in ((7, 0), (0, -2), (1, 2), (2, -1)):
        slot = Q_PLACE[dz, 1]
        arrived(qg.at[slot], qf_ss.at[i], qf_rs.at[i])
    wave(0, 4, 8)
    for i, dz in ((5, -3), (6, 3), (4, 4)):
        q_arrived(i, dz)
        q_pass(i, dz)
    wave(0, 8, 12)
    for i, dz in ((4, 4), (5, -3), (6, 3)):
        a_pass(i, dz)
    for i, dz in ((3, 1), (5, -3), (6, 3), (4, 4)):
        slot = Q_PLACE[dz, 1]
        arrived(qg.at[slot], qf_ss.at[i], qf_rs.at[i])
    wave(0, 12, 16)
    for g in (1, 2, 3):
        for slot in range(*GROUPS[g]):
            arrived(cg.at[slot], c_ss.at[slot], c_rs.at[slot])
        wave(g, 0, 16)
    m_groups = m_ref[0:4, :]
    m_tile = jnp.max(m_groups, axis=0, keepdims=True)
    l_tile = jnp.sum(l_ref[0:4, :] * jnp.exp2((m_groups - m_tile) * kk), axis=0, keepdims=True)

    places = [2 * ((z + dz) % NZ) + (core + dc) % 2 for dz, dc in Q_OFFSETS]

    def slot_rows(ref, start):
        return as_row([ref[pl.ds(start + place, 1), :] for place in places])

    for s, place in enumerate(places):
        st_own[pl.ds(place, 1), :] = m_tile[:, lanes_of(s)]
        st_own[pl.ds(SLOTS + place, 1), :] = l_tile[:, lanes_of(s)]
    send(st_own, st_sib, t_ss.at[0], t_rs.at[0], sibling)
    for s in range(SLOTS):
        qt[:, lanes_of(s)] = qg[s].T
    arrived(st_sib, t_ss.at[0], t_rs.at[0])
    m_a, m_b = st_own[0:SLOTS, :], st_sib[0:SLOTS, :]
    m_pair = jnp.maximum(m_a, m_b)
    l_pair = st_own[SLOTS:32, :] * jnp.exp2((m_a - m_pair) * kk)
    l_pair = l_pair + st_sib[SLOTS:32, :] * jnp.exp2((m_b - m_pair) * kk)
    st_all[z, 0:SLOTS, :] = m_pair
    st_all[z, SLOTS:32, :] = l_pair
    for d in (4, 3, 5, 2, 6, 1, 7):
        send(st_all.at[z], st_all.at[z], t_ss.at[d], t_rs.at[d], dev(0, 0, d, 0))

    m_pair_row = slot_rows(st_all.at[z], 0)
    shrink = jnp.exp2((m_groups - m_pair_row) * kk)
    own_class = [
        jnp.where((cc[b : b + 1, :] == class_of) & (slot_of == b), 1.0, 0.0).astype(BF16) for b in range(SLOTS)
    ]
    sums = jnp.dot(
        jnp.concatenate(own_class, axis=1), cg[...].reshape(TILE, D), preferred_element_type=F32
    )
    sums = jnp.concatenate(split2(sums), axis=0)

    def c_times_e(first):
        lanes = slice(first * ROWS, (first + 4) * ROWS)
        total = None
        for g, (start, stop) in enumerate(GROUPS):
            c_rows = cg[start:stop].reshape((stop - start) * ROWS, D)
            part = lax.dot_general(
                c_rows, e[start * ROWS : stop * ROWS, lanes], TN, preferred_element_type=F32
            )
            part = part * shrink[g : g + 1, lanes]
            total = part if total is None else total + part
        hits = lax.dot_general(sums, pt[:, lanes], TN, preferred_element_type=F32)
        return total, hits

    for half, first in enumerate((4, 12)):
        total, hits = c_times_e(first)
        for s in range(4):
            zs_sib[half, s, 0:D, :] = total[:, lanes_of(s)].astype(BF16)
            zs_sib[half, s, D : 2 * D, :] = hits[:, lanes_of(s)].astype(BF16)
        send(zs_sib.at[half], zr_sib.at[half], zb_ss.at[half], zb_rs.at[half], sibling)
    for half, first in enumerate((0, 8)):
        total, hits = c_times_e(first)
        for s in range(4):
            ot[4 * half + s] = total[:, lanes_of(s)]
            post[4 * half + s] = hits[:, lanes_of(s)]

    for i, dz in ((7, 0), (0, -2), (1, 2), (2, -1), (3, 1), (4, 4), (5, -3), (6, 3)):
        slot = Q_PLACE[dz, 1]
        arrived(aux.at[slot], af_ss.at[i], af_rs.at[i])
    cot = jnp.concatenate([aux[s, 0:1, :] for s in range(SLOTS)], axis=0)
    coef_pos = cot * per_count
    weights = [
        jnp.where((rc[s : s + 1, :] == class_of) & (slot_of == s), -coef_pos[s : s + 1, :], 0.0)
        for s in range(SLOTS)
    ]
    weights = jnp.concatenate(split2(jnp.concatenate(weights, axis=1)), axis=0)
    sums_q = jnp.dot(weights, qg[...].reshape(TILE, D), preferred_element_type=F32)
    sums_q = sums_q[0:ROWS, :] + sums_q[ROWS:NB, :]
    sums_q = jnp.concatenate(split2(sums_q), axis=0)
    soft_row = as_row([(count * per_count)[s : s + 1, :] for s in range(SLOTS)])
    cot_row = as_row([cot[s : s + 1, :] for s in range(SLOTS)])

    for d in (1, 7, 2, 6, 3, 5, 4):
        slot = (z - d + NZ) % NZ
        arrived(st_all.at[slot], t_ss.at[d], t_rs.at[d])
    m_all = st_all[0, 0:SLOTS, :]
    for s in range(1, NZ):
        m_all = jnp.maximum(m_all, st_all[s, 0:SLOTS, :])
    l_all = jnp.zeros((SLOTS, ROWS), F32)
    for s in range(NZ):
        l_all = l_all + st_all[s, SLOTS:32, :] * jnp.exp2((st_all[s, 0:SLOTS, :] - m_all) * kk)
    st_end[0:SLOTS, :] = m_all
    st_end[SLOTS:32, :] = 1.0 / l_all
    top_row, per_mass = slot_rows(st_end, 0), slot_rows(st_end, SLOTS)
    soft_row = soft_row * per_mass
    a_groups = soft_row * cot_row * jnp.exp2((m_groups - top_row) * kk)
    a_pair = soft_row * jnp.exp2((m_pair_row - top_row) * kk)

    def dc_group(g):
        first, last = GROUPS[g]
        rows = slice(first * ROWS, last * ROWS)
        aqt[g % 2] = (qt[...].astype(F32) * a_groups[g : g + 1, :]).astype(BF16)
        part = lax.dot_general(e[rows, :], aqt[g % 2], NT, preferred_element_type=F32)
        part = part + jnp.dot(pc[rows, :], sums_q, preferred_element_type=F32)
        dcf[first:last] = part.reshape(last - first, ROWS, D)

    hub = {2: 0, 1: 1, 3: 2}

    def dc_send(slot):
        a, b = OFFSETS[slot]
        i = slot - 7
        odd = (par + a + b) % 2
        xs1[i] = dcf[slot].astype(BF16)
        even_to = hub[a] * 3 + (-b) % NY - 1
        odd_to = hub[b] * 3 + (-a) % NX - 1
        there = even_to + odd * (odd_to - even_to)
        send(xs1.at[i], xr1.at[there], x1_ss.at[i], x1_rs.at[there], dev(odd * a, (1 - odd) * b, 0, 0))

    dc_group(3)
    for slot in (15, 13, 14):
        dc_send(slot)

    for half in range(2):
        arrived(zr_sib.at[half], zb_ss.at[half], zb_rs.at[half])
    for i, s in enumerate(OWN_CORE):
        lanes = lanes_of(s)
        half, j = i // 4, i % 4
        soft = ot[i] + zr_sib[half, j, 0:D, :].astype(F32)
        hits = post[i] + zr_sib[half, j, D : 2 * D, :].astype(F32)
        zp[i] = soft * a_pair[:, lanes] - hits * per_count[s : s + 1, :]

    def z_part(dz):
        return OWN_CORE.index(Q_PLACE[dz, 0])

    for i, (target, hop) in enumerate(((-3, -1), (3, 1), (4, -2 * zsig))):
        zs1[i] = zp[z_part(target)].astype(BF16)
        send(zs1.at[i], zr1.at[i], z1_ss.at[i], z1_rs.at[i], dev(0, 0, hop, 0))
    for i, target in ((2, -1), (3, 1)):
        zs2[i] = zp[z_part(target)].astype(BF16)
        send(zs2.at[i], zr2.at[i], z2_ss.at[i], z2_rs.at[i], dev(0, 0, target, 0))

    dc_group(2)
    for slot in (11, 12, 10):
        dc_send(slot)
    dc_group(1)
    for slot in (7, 8, 9):
        dc_send(slot)
    dc_group(0)
    for i, (slot, there, even, odd) in enumerate(
        (
            (c_slot(6, 3), c_slot(6, 3), (0, 2), (2, 0)),
            (c_slot(1, 4), c_slot(2, 5), (1, 0), (0, 1)),
            (c_slot(2, 5), c_slot(1, 4), (3, 0), (0, 3)),
        )
    ):
        xs2[i] = dcf[slot].astype(BF16)
        to = dev(even[0] + par * (odd[0] - even[0]), even[1] + par * (odd[1] - even[1]), 0, 0)
        send(xs2.at[i], xr2.at[there - 1], x2_ss.at[i], x2_rs.at[there - 1], to)

    for i in range(3):
        arrived(zr1.at[i], z1_ss.at[i], z1_rs.at[i])
    far = zr1[2].astype(F32)
    down = zp[z_part(-2)] + zr1[0].astype(F32) + jnp.where(zpar == 0, far, 0.0)
    up = zp[z_part(2)] + zr1[1].astype(F32) + jnp.where(zpar == 1, far, 0.0)
    zs2[0] = down.astype(BF16)
    zs2[1] = up.astype(BF16)
    send(zs2.at[0], zr2.at[0], z2_ss.at[0], z2_rs.at[0], dev(0, 0, -2, 0))
    send(zs2.at[1], zr2.at[1], z2_ss.at[1], z2_rs.at[1], dev(0, 0, 2, 0))

    for j, (slot, there, even, odd) in enumerate(
        (
            (c_slot(3, 6), c_slot(3, 6), (2, 0), (0, 2)),
            (c_slot(4, 1), c_slot(5, 2), (0, 1), (1, 0)),
            (c_slot(5, 2), c_slot(4, 1), (0, 3), (3, 0)),
        )
    ):
        total = dcf[slot]
        for d in range(3):
            arrived(xr1.at[3 * j + d], x1_ss.at[3 * j + d], x1_rs.at[3 * j + d])
            total = total + xr1[3 * j + d].astype(F32)
        xs2[3 + j] = total.astype(BF16)
        to = dev(even[0] + par * (odd[0] - even[0]), even[1] + par * (odd[1] - even[1]), 0, 0)
        send(xs2.at[3 + j], xr2.at[there - 1], x2_ss.at[3 + j], x2_rs.at[there - 1], to)

    total = zp[0]
    for i in (2, 3, 0, 1):
        arrived(zr2.at[i], z2_ss.at[i], z2_rs.at[i])
        total = total + zr2[i].astype(F32)
    dq_out[...] = (total * cot[0:1, :]).T
    total = dcf[0]
    for i in range(6):
        arrived(xr2.at[i], x2_ss.at[i], x2_rs.at[i])
        total = total + xr2[i].astype(F32)
    dc_out[...] = total
    for copy in pending:
        copy.wait_send()


def shards(queries, candidates, block_mask, row_class, col_class, cotangent):
    dma = pltpu.SemaphoreType.DMA
    vmem = pltpu.VMEM
    block = (D, ROWS)
    scratch = [
        vmem((NB, NB), jnp.int32),
        vmem((NB, ROWS), jnp.int32),
        vmem((NB, ROWS), jnp.int32),
        vmem((NX, ROWS), F32),
        vmem((SLOTS, 8, ROWS), F32),
        vmem((SLOTS, ROWS, D), BF16),
        vmem((SLOTS, ROWS, D), BF16),
        vmem((D, TILE), BF16),
        vmem((TILE, TILE), BF16),
        vmem((8, TILE), F32),
        vmem((8, TILE), F32),
        vmem((NB, TILE), BF16),
        vmem((TILE, NB), BF16),
        vmem((8,) + block, F32),
        vmem((8,) + block, F32),
        vmem((32, ROWS), F32),
        vmem((32, ROWS), F32),
        vmem((NZ, 32, ROWS), F32),
        vmem((32, ROWS), F32),
        vmem((2, D, TILE), BF16),
        vmem((SLOTS, ROWS, D), F32),
        vmem((2, 4, 2 * D, ROWS), BF16),
        vmem((2, 4, 2 * D, ROWS), BF16),
        vmem((8,) + block, F32),
        vmem((3,) + block, BF16),
        vmem((3,) + block, BF16),
        vmem((4,) + block, BF16),
        vmem((4,) + block, BF16),
        vmem((9, ROWS, D), BF16),
        vmem((9, ROWS, D), BF16),
        vmem((6, ROWS, D), BF16),
        vmem((6, ROWS, D), BF16),
        dma((6,)),
        dma((7,)), dma((7,)), dma((8,)), dma((8,)), dma((7,)), dma((7,)), dma((8,)), dma((8,)),
        dma((16,)), dma((16,)), dma((8,)), dma((8,)), dma((2,)), dma((2,)),
        dma((3,)), dma((3,)), dma((4,)), dma((4,)), dma((9,)), dma((9,)), dma((6,)), dma((6,)),
    ]
    out = vmem((ROWS, D), F32)
    dq, dc = pl.pallas_call(
        kernel,
        out_shape=(out, out),
        in_specs=[pl.BlockSpec(memory_space=pl.ANY)] * 6,
        out_specs=(pl.BlockSpec(memory_space=vmem), pl.BlockSpec(memory_space=vmem)),
        scratch_shapes=scratch,
        compiler_params=pltpu.CompilerParams(
            collective_id=0, has_side_effects=True, vmem_limit_bytes=56 * 2**20
        ),
    )(
        queries,
        candidates,
        block_mask,
        row_class.reshape(NB, ROWS),
        col_class.reshape(NB, ROWS),
        cotangent.reshape(NX, ROWS),
    )
    scale = 1.0 / math.sqrt(D)
    return dq * scale, dc * scale


def solution(mesh):
    in_specs = (P(("row", "col"), None), P(("row", "col"), None), P(), P(), P(), P("row"))
    out_specs = (P(("row", "col"), None), P(("row", "col"), None))
    return jax.shard_map(shards, mesh=mesh, in_specs=in_specs, out_specs=out_specs, check_vma=False)
```

```python
import math

import jax
import jax.numpy as jnp
from jax import lax
from jax.experimental import pallas as pl
from jax.experimental.pallas import tpu as pltpu
from jax.sharding import PartitionSpec as P

MESH = pl.DeviceIdType.MESH
F32 = jnp.float32
BF16 = jnp.bfloat16
ROWS = 128
D = 256
NX, NY, NZ = 4, 4, 8
TILE = 2048
SLOTS = 16
CLASSES = 8
NB = 256
LOG2E = math.log2(math.e)
NT = (((1,), (1,)), ((), ()))
TN = (((0,), (0,)), ((), ()))

OFFSETS = [(0, 0), (1, 0), (3, 0), (2, 0), (0, 1), (0, 3), (0, 2)]
OFFSETS += [(1, 1), (1, 3), (3, 1), (3, 3), (1, 2), (3, 2), (2, 1), (2, 3), (2, 2)]
PLACE = {o: i for i, o in enumerate(OFFSETS)}
GROUPS = ((0, 7), (7, 11), (11, 16))
Q_OFFSETS = [(0, 0), (-2, 0), (2, 0), (-1, 0), (0, 1), (-2, 1), (2, 1), (-1, 1)]
Q_OFFSETS += [(1, 0), (4, 0), (-3, 0), (3, 0), (1, 1), (4, 1), (-3, 1), (3, 1)]
Q_PLACE = {o: i for i, o in enumerate(Q_OFFSETS)}
OWN_CORE = (0, 1, 2, 3, 8, 9, 10, 11)


def split2(value):
    high = value.astype(BF16)
    return high, (value - high.astype(F32)).astype(BF16)


def as_row(rows):
    return jnp.concatenate(rows, axis=1)


def lanes_of(slot):
    return slice(slot * ROWS, (slot + 1) * ROWS)


def kernel(
    q_own, c_own, mask_hbm, rc_hbm, cc_hbm, cot_hbm, dq_out, dc_out,
    mask_ref, rc_ref, cc_ref, cot_ref, aux,
    qg, cg, qt, e, m_ref, l_ref, pt, pc, ot, post, st_own, st_sib, st_all, st_end, aqt,
    dcf, zs_sib, zr_sib, zp, zs1, zr1, zs2, zr2, xs1, xr1, xs2, xr2, xs3, xr3,
    in_s, q_ss, q_rs, qf_ss, qf_rs, a_ss, a_rs, af_ss, af_rs, c_ss, c_rs, t_ss, t_rs, zb_ss, zb_rs,
    z1_ss, z1_rs, z2_ss, z2_rs, x1_ss, x1_rs, x2_ss, x2_rs, x3_ss, x3_rs,
):
    kk = LOG2E / math.sqrt(D)
    x = lax.axis_index("col")
    row = lax.axis_index("row")
    core = row % 2
    z = (row // 2) % NZ
    y = row // (2 * NZ)
    par = (x + y) % 2
    zpar = z % 2
    zsig = 1 - 2 * zpar

    def dev(dx, dy, dz, dcore):
        ny, nz, nc = (y + dy) % NY, (z + dz) % NZ, (core + dcore) % 2
        return ((ny * NZ + nz) * 2 + nc, (x + dx) % NX)

    sibling = dev(0, 0, 0, 1)
    pending = []

    def send(src, dst, ssem, rsem, to):
        copy = pltpu.make_async_remote_copy(
            src_ref=src, dst_ref=dst, send_sem=ssem, recv_sem=rsem, device_id=to, device_id_type=MESH
        )
        copy.start()
        pending.append(copy)

    def arrived(dst, ssem, rsem):
        pltpu.make_async_remote_copy(
            src_ref=dst, dst_ref=dst, send_sem=ssem, recv_sem=rsem, device_id=sibling, device_id_type=MESH
        ).wait_recv()

    barrier = pltpu.get_barrier_semaphore()
    peers = [dev(0, 0, d, 0) for d in (2, 6, 1, 7)]
    peers += [dev(d, 0, 0, 0) for d in (2, 1, 3)]
    peers += [dev(0, d, 0, 0) for d in (2, 1, 3)]
    peers += [sibling]
    for peer in peers:
        pl.semaphore_signal(barrier, inc=1, device_id=peer, device_id_type=MESH)
    loads = [
        pltpu.make_async_copy(src, dst, in_s.at[i])
        for i, (src, dst) in enumerate(
            (
                (cot_hbm, cot_ref), (mask_hbm, mask_ref), (rc_hbm, rc_ref), (cc_hbm, cc_ref),
                (q_own, qg.at[0]), (c_own, cg.at[0]),
            )
        )
    ]
    for load in loads:
        load.start()
    pl.semaphore_wait(barrier, len(peers))

    z_hops = (2, -2, 1, -1)
    for i, hop in enumerate(z_hops):
        send(q_own, qg.at[Q_PLACE[-hop, 0]], q_ss.at[i], q_rs.at[i], dev(0, 0, hop, 0))
    for o in OFFSETS[1:7]:
        back = PLACE[(-o[0]) % NX, (-o[1]) % NY]
        send(c_own, cg.at[back], c_ss.at[back], c_rs.at[back], dev(o[0], o[1], 0, 0))
    send(q_own, qg.at[Q_PLACE[0, 1]], qf_ss.at[7], qf_rs.at[7], sibling)
    for load in loads:
        load.wait()
    aux[0] = jnp.broadcast_to(cot_ref[pl.ds(x, 1), :], (8, ROWS))
    for i, hop in enumerate(z_hops):
        send(aux.at[0], aux.at[Q_PLACE[-hop, 0]], a_ss.at[i], a_rs.at[i], dev(0, 0, hop, 0))
    send(aux.at[0], aux.at[Q_PLACE[0, 1]], af_ss.at[7], af_rs.at[7], sibling)

    lane256 = lax.broadcasted_iota(jnp.int32, (SLOTS, NB), 1)
    slot256 = lax.broadcasted_iota(jnp.int32, (SLOTS, NB), 0)
    q_block = jnp.zeros((SLOTS, NB), jnp.int32)
    for s, (dz, dc) in enumerate(Q_OFFSETS):
        block = ((y * NZ + (z + dz) % NZ) * 2 + (core + dc) % 2) * NX + x
        q_block = jnp.where(slot256 == s, block, q_block)
    sel_q = jnp.where(lane256 == q_block, 1.0, 0.0).astype(BF16)
    c_block = jnp.zeros((SLOTS, NB), jnp.int32)
    for b, (dx, dy) in enumerate(OFFSETS):
        block = ((((y + dy) % NY) * NZ + z) * 2 + core) * NX + (x + dx) % NX
        c_block = jnp.where(slot256 == b, block, c_block)
    sel_c = jnp.where(lane256 == c_block, 1.0, 0.0).astype(BF16)
    mask = mask_ref[...].astype(F32).astype(BF16)
    rc_all = rc_ref[...].astype(F32).astype(BF16)
    cc_all = cc_ref[...].astype(F32)
    m_sel = jnp.dot(sel_q, mask, preferred_element_type=F32).astype(BF16)
    rc = jnp.dot(sel_q, rc_all, preferred_element_type=F32)
    cc = jnp.dot(sel_c, cc_all.astype(BF16), preferred_element_type=F32)
    lane128 = lax.broadcasted_iota(jnp.int32, (ROWS, ROWS), 1)
    hist = jnp.zeros((NB, ROWS), F32)
    for k in range(CLASSES):
        column = jnp.where(lane128 == k, 1.0, 0.0).astype(BF16)
        same = jnp.where(cc_all == float(k), 1.0, 0.0).astype(BF16)
        hist = hist + jnp.dot(same, column, preferred_element_type=F32)
    per_class = jnp.dot(m_sel, hist.astype(BF16), preferred_element_type=F32)
    count = jnp.zeros((SLOTS, ROWS), F32)
    for k in range(CLASSES):
        count = jnp.where(rc == float(k), per_class[:, k : k + 1], count)
    per_count = 1.0 / jnp.maximum(count, 1.0)
    class_of = (lax.broadcasted_iota(jnp.int32, (ROWS, ROWS), 0) % CLASSES).astype(F32)
    slot_of = lax.broadcasted_iota(jnp.int32, (ROWS, ROWS), 0) // CLASSES

    def repeated(value):
        return jnp.broadcast_to(value[:, None, :], (SLOTS, CLASSES, NB)).reshape(ROWS, NB)

    sel_c_rows = repeated(sel_c.astype(F32)).astype(BF16)
    m_sel_rows = repeated(m_sel.astype(F32)).astype(BF16)
    hit_q = lax.dot_general(sel_c_rows, m_sel, NT, preferred_element_type=F32)
    hit_c = lax.dot_general(m_sel_rows, sel_c, NT, preferred_element_type=F32)
    for s in range(SLOTS):
        picked = jnp.where(rc[s : s + 1, :] == class_of, hit_q[:, s : s + 1], 0.0).astype(BF16)
        pt[0:ROWS, lanes_of(s)] = picked
        pt[ROWS:NB, lanes_of(s)] = picked
        picked = jnp.where(cc[s : s + 1, :] == class_of, hit_c[:, s : s + 1], 0.0).T.astype(BF16)
        pc[lanes_of(s), 0:ROWS] = picked
        pc[lanes_of(s), ROWS:NB] = picked

    def c_slot(even, odd):
        return even + par * (odd - even)

    turn = [
        (c_slot(4, 1), 1 - par, par, [((d, 0), (0, d)) for d in (1, 3, 2)], ((0, 1), (1, 0))),
        (c_slot(5, 2), 1 - par, par, [((d, 0), (0, d)) for d in (1, 3, 2)], ((0, 3), (3, 0))),
        (c_slot(3, 6), par, 1 - par, [((0, d), (d, 0)) for d in (1, 3, 2)], ((2, 0), (0, 2))),
    ]
    forwards = [0]

    def c_forward(slot, fx, fy, hops, origin):
        arrived(cg.at[slot], c_ss.at[slot], c_rs.at[slot])
        for even, odd in hops:
            d = max(even)
            there = [
                PLACE[((o[0] - h[0]) % NX, (o[1] - h[1]) % NY)] for o, h in zip(origin, (even, odd))
            ]
            there = c_slot(*there)
            i = 7 + forwards[0]
            send(cg.at[slot], cg.at[there], c_ss.at[i], c_rs.at[there], dev(fx * d, fy * d, 0, 0))
            forwards[0] += 1

    def q_arrived(i, dz):
        slot = Q_PLACE[dz, 0]
        arrived(qg.at[slot], q_ss.at[i], q_rs.at[i])

    def q_pass(i, dz):
        here, there = Q_PLACE[dz, 0], Q_PLACE[dz, 1]
        send(qg.at[here], qg.at[there], qf_ss.at[i], qf_rs.at[i], sibling)

    def a_pass(i, dz):
        here, there = Q_PLACE[dz, 0], Q_PLACE[dz, 1]
        arrived(aux.at[here], a_ss.at[i], a_rs.at[i])
        send(aux.at[here], aux.at[there], af_ss.at[i], af_rs.at[i], sibling)

    def onward(ref, ss, rs):
        far = Q_PLACE[-2, 0] + zpar * (Q_PLACE[2, 0] - Q_PLACE[-2, 0])
        send(ref.at[far], ref.at[Q_PLACE[4, 0]], ss.at[4], rs.at[4], dev(0, 0, 2 * zsig, 0))
        send(ref.at[Q_PLACE[-2, 0]], ref.at[Q_PLACE[-3, 0]], ss.at[5], rs.at[5], dev(0, 0, 1, 0))
        send(ref.at[Q_PLACE[2, 0]], ref.at[Q_PLACE[3, 0]], ss.at[6], rs.at[6], dev(0, 0, -1, 0))

    c_forward(*turn[0])
    c_forward(*turn[1])
    q_arrived(0, -2)
    q_arrived(1, 2)
    onward(qg, q_ss, q_rs)
    c_forward(*turn[2])
    q_pass(0, -2)
    q_pass(1, 2)
    q_arrived(2, -1)
    q_pass(2, -1)
    q_arrived(3, 1)
    q_pass(3, 1)
    a_pass(0, -2)
    a_pass(1, 2)
    a_pass(2, -1)
    a_pass(3, 1)
    onward(aux, a_ss, a_rs)
    for slot in (c_slot(1, 4), c_slot(2, 5), c_slot(6, 3)):
        arrived(cg.at[slot], c_ss.at[slot], c_rs.at[slot])

    def wave(g, q_first, q_last):
        first, last = GROUPS[g]
        rows = slice(first * ROWS, last * ROWS)
        lanes = slice(q_first * ROWS, q_last * ROWS)
        c_rows = cg[first:last].reshape((last - first) * ROWS, D)
        q_rows = qg[q_first:q_last].reshape((q_last - q_first) * ROWS, D)
        scores = lax.dot_general(c_rows, q_rows, NT, preferred_element_type=F32)
        top = jnp.max(scores, axis=0, keepdims=True)
        grown = jnp.exp2((scores - top) * kk)
        m_ref[g : g + 1, lanes] = top * kk
        l_ref[g : g + 1, lanes] = jnp.sum(grown, axis=0, keepdims=True)
        e[rows, lanes] = grown.astype(BF16)

    def c_wait(g):
        for slot in range(*GROUPS[g]):
            arrived(cg.at[slot], c_ss.at[slot], c_rs.at[slot])

    wave(0, 0, 4)
    for i, dz in ((7, 0), (0, -2), (1, 2), (2, -1)):
        slot = Q_PLACE[dz, 1]
        arrived(qg.at[slot], qf_ss.at[i], qf_rs.at[i])
    wave(0, 4, 8)
    c_wait(1)
    wave(1, 0, 8)
    for i, dz in ((5, -3), (6, 3), (4, 4)):
        q_arrived(i, dz)
        q_pass(i, dz)
    wave(0, 8, 12)
    wave(1, 8, 12)
    for i, dz in ((4, 4), (5, -3), (6, 3)):
        a_pass(i, dz)
    c_wait(2)
    wave(2, 0, 12)
    for i, dz in ((3, 1), (5, -3), (6, 3), (4, 4)):
        slot = Q_PLACE[dz, 1]
        arrived(qg.at[slot], qf_ss.at[i], qf_rs.at[i])
    for g in range(3):
        wave(g, 12, 16)
    tops = m_ref[0:3, :]
    top_tile = jnp.max(tops, axis=0, keepdims=True)
    mass = jnp.sum(l_ref[0:3, :] * jnp.exp2(tops - top_tile), axis=0, keepdims=True)
    log_tile = top_tile + jnp.log2(mass)

    places = [2 * ((z + dz) % NZ) + (core + dc) % 2 for dz, dc in Q_OFFSETS]

    def slot_rows(ref):
        return as_row([ref[pl.ds(place, 1), :] for place in places])

    for s, place in enumerate(places):
        st_own[pl.ds(place, 1), :] = log_tile[:, lanes_of(s)]
    send(st_own, st_sib, t_ss.at[0], t_rs.at[0], sibling)
    for s in range(SLOTS):
        qt[:, lanes_of(s)] = qg[s].T
    arrived(st_sib, t_ss.at[0], t_rs.at[0])
    log_a, log_b = st_own[...], st_sib[...]
    top = jnp.maximum(log_a, log_b)
    st_all[z] = top + jnp.log2(jnp.exp2(log_a - top) + jnp.exp2(log_b - top))
    for d in (4, 3, 5, 2, 6, 1, 7):
        send(st_all.at[z], st_all.at[z], t_ss.at[d], t_rs.at[d], dev(0, 0, d, 0))

    log_pair = slot_rows(st_all.at[z])
    shrink = jnp.exp2(tops - log_pair)
    own_class = [
        jnp.where((cc[b : b + 1, :] == class_of) & (slot_of == b), 1.0, 0.0).astype(BF16) for b in range(SLOTS)
    ]
    sums = jnp.dot(
        jnp.concatenate(own_class, axis=1), cg[...].reshape(TILE, D), preferred_element_type=F32
    )
    sums = jnp.concatenate(split2(sums), axis=0)

    def c_times_e(first):
        lanes = slice(first * ROWS, (first + 4) * ROWS)
        total = None
        for g, (start, stop) in enumerate(GROUPS):
            c_rows = cg[start:stop].reshape((stop - start) * ROWS, D)
            part = lax.dot_general(
                c_rows, e[start * ROWS : stop * ROWS, lanes], TN, preferred_element_type=F32
            )
            part = part * shrink[g : g + 1, lanes]
            total = part if total is None else total + part
        hits = lax.dot_general(sums, pt[:, lanes], TN, preferred_element_type=F32)
        return total, hits

    for half, first in enumerate((4, 12)):
        total, hits = c_times_e(first)
        for s in range(4):
            zs_sib[half, s, 0:D, :] = total[:, lanes_of(s)].astype(BF16)
            zs_sib[half, s, D : 2 * D, :] = hits[:, lanes_of(s)].astype(BF16)
        send(zs_sib.at[half], zr_sib.at[half], zb_ss.at[half], zb_rs.at[half], sibling)
    for half, first in enumerate((0, 8)):
        total, hits = c_times_e(first)
        for s in range(4):
            ot[4 * half + s] = total[:, lanes_of(s)]
            post[4 * half + s] = hits[:, lanes_of(s)]

    for i, dz in ((7, 0), (0, -2), (1, 2), (2, -1), (3, 1), (4, 4), (5, -3), (6, 3)):
        slot = Q_PLACE[dz, 1]
        arrived(aux.at[slot], af_ss.at[i], af_rs.at[i])
    cot = jnp.concatenate([aux[s, 0:1, :] for s in range(SLOTS)], axis=0)
    coef_pos = cot * per_count
    weights = [
        jnp.where((rc[s : s + 1, :] == class_of) & (slot_of == s), -coef_pos[s : s + 1, :], 0.0)
        for s in range(SLOTS)
    ]
    weights = jnp.concatenate(split2(jnp.concatenate(weights, axis=1)), axis=0)
    sums_q = jnp.dot(weights, qg[...].reshape(TILE, D), preferred_element_type=F32)
    sums_q = sums_q[0:ROWS, :] + sums_q[ROWS:NB, :]
    sums_q = jnp.concatenate(split2(sums_q), axis=0)
    soft_row = as_row([(count * per_count)[s : s + 1, :] for s in range(SLOTS)])
    cot_row = as_row([cot[s : s + 1, :] for s in range(SLOTS)])

    for d in (1, 7, 2, 6, 3, 5, 4):
        slot = (z - d + NZ) % NZ
        arrived(st_all.at[slot], t_ss.at[d], t_rs.at[d])
    top = st_all[0]
    for s in range(1, NZ):
        top = jnp.maximum(top, st_all[s])
    mass = jnp.zeros((SLOTS, ROWS), F32)
    for s in range(NZ):
        mass = mass + jnp.exp2(st_all[s] - top)
    st_end[0] = top
    st_end[1] = 1.0 / mass
    top_row = slot_rows(st_end.at[0])
    soft_row = soft_row * slot_rows(st_end.at[1])
    a_groups = soft_row * cot_row * jnp.exp2(tops - top_row)
    a_pair = soft_row * jnp.exp2(log_pair - top_row)

    def z_part(dz):
        return OWN_CORE.index(Q_PLACE[dz, 0])

    def z_sum(i):
        s = OWN_CORE[i]
        half, j = i // 4, i % 4
        soft = ot[i] + zr_sib[half, j, 0:D, :].astype(F32)
        hits = post[i] + zr_sib[half, j, D : 2 * D, :].astype(F32)
        return soft * a_pair[:, lanes_of(s)] - hits * per_count[s : s + 1, :]

    for half in range(2):
        arrived(zr_sib.at[half], zb_ss.at[half], zb_rs.at[half])
    for i, (target, hop) in enumerate(((4, -2 * zsig), (-3, -1), (3, 1))):
        zs1[i] = z_sum(z_part(target)).astype(BF16)
        send(zs1.at[i], zr1.at[i], z1_ss.at[i], z1_rs.at[i], dev(0, 0, hop, 0))

    def dc_group(g):
        first, last = GROUPS[g]
        rows = slice(first * ROWS, last * ROWS)
        aqt[g % 2] = (qt[...].astype(F32) * a_groups[g : g + 1, :]).astype(BF16)
        part = lax.dot_general(e[rows, :], aqt[g % 2], NT, preferred_element_type=F32)
        part = part + jnp.dot(pc[rows, :], sums_q, preferred_element_type=F32)
        dcf[first:last] = part.reshape(last - first, ROWS, D)

    hub = {2: 0, 1: 1, 3: 2}

    def dc_send(slot):
        a, b = OFFSETS[slot]
        i = slot - 11
        odd = (par + a + b) % 2
        xs1[i] = dcf[slot].astype(BF16)
        even_to = hub[a] * 3 + (-b) % NY - 1
        odd_to = hub[b] * 3 + (-a) % NX - 1
        there = even_to + odd * (odd_to - even_to)
        send(xs1.at[i], xr1.at[there], x1_ss.at[i], x1_rs.at[there], dev(odd * a, (1 - odd) * b, 0, 0))

    dc_group(2)
    for slot in (15, 11, 12, 13, 14):
        dc_send(slot)
    for i, target in ((2, -1), (3, 1)):
        zs2[i] = z_sum(z_part(target)).astype(BF16)
        send(zs2.at[i], zr2.at[i], z2_ss.at[i], z2_rs.at[i], dev(0, 0, target, 0))
    dc_group(1)
    for slot in range(7, 11):
        a, b = OFFSETS[slot]
        back = PLACE[(-a) % NX, (-b) % NY] - 7
        xs3[slot - 7] = dcf[slot].astype(BF16)
        send(xs3.at[slot - 7], xr3.at[back], x3_ss.at[back], x3_rs.at[back], dev(a, b, 0, 0))
    for target in (0, -2, 2):
        zp[z_part(target)] = z_sum(z_part(target))
    dc_group(0)
    for i, (slot, there, even, odd) in enumerate(
        (
            (c_slot(6, 3), c_slot(6, 3), (0, 2), (2, 0)),
            (c_slot(1, 4), c_slot(2, 5), (1, 0), (0, 1)),
            (c_slot(2, 5), c_slot(1, 4), (3, 0), (0, 3)),
        )
    ):
        xs2[i] = dcf[slot].astype(BF16)
        to = dev(even[0] + par * (odd[0] - even[0]), even[1] + par * (odd[1] - even[1]), 0, 0)
        send(xs2.at[i], xr2.at[there - 1], x2_ss.at[i], x2_rs.at[there - 1], to)

    for i in range(3):
        arrived(zr1.at[i], z1_ss.at[i], z1_rs.at[i])
    far = zr1[0].astype(F32)
    down = zp[z_part(-2)] + zr1[1].astype(F32) + jnp.where(zpar == 0, far, 0.0)
    up = zp[z_part(2)] + zr1[2].astype(F32) + jnp.where(zpar == 1, far, 0.0)
    zs2[0] = down.astype(BF16)
    zs2[1] = up.astype(BF16)
    send(zs2.at[0], zr2.at[0], z2_ss.at[0], z2_rs.at[0], dev(0, 0, -2, 0))
    send(zs2.at[1], zr2.at[1], z2_ss.at[1], z2_rs.at[1], dev(0, 0, 2, 0))

    for j, (slot, there, even, odd) in enumerate(
        (
            (c_slot(3, 6), c_slot(3, 6), (2, 0), (0, 2)),
            (c_slot(4, 1), c_slot(5, 2), (0, 1), (1, 0)),
            (c_slot(5, 2), c_slot(4, 1), (0, 3), (3, 0)),
        )
    ):
        total = dcf[slot]
        for d in range(3) if j == 0 else (1,):
            arrived(xr1.at[3 * j + d], x1_ss.at[0], x1_rs.at[3 * j + d])
            total = total + xr1[3 * j + d].astype(F32)
        xs2[3 + j] = total.astype(BF16)
        to = dev(even[0] + par * (odd[0] - even[0]), even[1] + par * (odd[1] - even[1]), 0, 0)
        send(xs2.at[3 + j], xr2.at[there - 1], x2_ss.at[3 + j], x2_rs.at[there - 1], to)

    total = zp[0]
    for i in (2, 3, 0, 1):
        arrived(zr2.at[i], z2_ss.at[i], z2_rs.at[i])
        total = total + zr2[i].astype(F32)
    dq_out[...] = (total * cot[0:1, :]).T
    total = dcf[0]
    for i in range(6):
        arrived(xr2.at[i], x2_ss.at[i], x2_rs.at[i])
        total = total + xr2[i].astype(F32)
    for i in range(4):
        arrived(xr3.at[i], x3_ss.at[i], x3_rs.at[i])
        total = total + xr3[i].astype(F32)
    dc_out[...] = total
    for copy in pending:
        copy.wait_send()


def shards(queries, candidates, block_mask, row_class, col_class, cotangent):
    dma = pltpu.SemaphoreType.DMA
    vmem = pltpu.VMEM
    block = (D, ROWS)
    scratch = [
        vmem((NB, NB), jnp.int32),
        vmem((NB, ROWS), jnp.int32),
        vmem((NB, ROWS), jnp.int32),
        vmem((NX, ROWS), F32),
        vmem((SLOTS, 8, ROWS), F32),
        vmem((SLOTS, ROWS, D), BF16),
        vmem((SLOTS, ROWS, D), BF16),
        vmem((D, TILE), BF16),
        vmem((TILE, TILE), BF16),
        vmem((8, TILE), F32),
        vmem((8, TILE), F32),
        vmem((NB, TILE), BF16),
        vmem((TILE, NB), BF16),
        vmem((8,) + block, F32),
        vmem((8,) + block, F32),
        vmem((SLOTS, ROWS), F32),
        vmem((SLOTS, ROWS), F32),
        vmem((NZ, SLOTS, ROWS), F32),
        vmem((2, SLOTS, ROWS), F32),
        vmem((2, D, TILE), BF16),
        vmem((SLOTS, ROWS, D), F32),
        vmem((2, 4, 2 * D, ROWS), BF16),
        vmem((2, 4, 2 * D, ROWS), BF16),
        vmem((8,) + block, F32),
        vmem((3,) + block, BF16),
        vmem((3,) + block, BF16),
        vmem((4,) + block, BF16),
        vmem((4,) + block, BF16),
        vmem((5, ROWS, D), BF16),
        vmem((9, ROWS, D), BF16),
        vmem((6, ROWS, D), BF16),
        vmem((6, ROWS, D), BF16),
        vmem((4, ROWS, D), BF16),
        vmem((4, ROWS, D), BF16),
        dma((6,)),
        dma((7,)), dma((7,)), dma((8,)), dma((8,)), dma((7,)), dma((7,)), dma((8,)), dma((8,)),
        dma((16,)), dma((16,)), dma((8,)), dma((8,)), dma((2,)), dma((2,)),
        dma((3,)), dma((3,)), dma((4,)), dma((4,)), dma((5,)), dma((9,)), dma((6,)), dma((6,)), dma((4,)), dma((4,)),
    ]
    out = vmem((ROWS, D), F32)
    dq, dc = pl.pallas_call(
        kernel,
        out_shape=(out, out),
        in_specs=[pl.BlockSpec(memory_space=pl.ANY)] * 6,
        out_specs=(pl.BlockSpec(memory_space=vmem), pl.BlockSpec(memory_space=vmem)),
        scratch_shapes=scratch,
        compiler_params=pltpu.CompilerParams(
            collective_id=0, has_side_effects=True, vmem_limit_bytes=56 * 2**20
        ),
    )(
        queries,
        candidates,
        block_mask,
        row_class.reshape(NB, ROWS),
        col_class.reshape(NB, ROWS),
        cotangent.reshape(NX, ROWS),
    )
    scale = 1.0 / math.sqrt(D)
    return dq * scale, dc * scale


def solution(mesh):
    in_specs = (P(("row", "col"), None), P(("row", "col"), None), P(), P(), P(), P("row"))
    out_specs = (P(("row", "col"), None), P(("row", "col"), None))
    return jax.shard_map(shards, mesh=mesh, in_specs=in_specs, out_specs=out_specs, check_vma=False)
```

```python
import math

import jax
import jax.numpy as jnp
from jax import lax
from jax.experimental import pallas as pl
from jax.experimental.pallas import tpu as pltpu
from jax.sharding import PartitionSpec as P

MESH = pl.DeviceIdType.MESH
F32 = jnp.float32
BF16 = jnp.bfloat16
ROWS = 128
D = 256
NX, NY, NZ = 4, 4, 8
TILE = 2048
SLOTS = 16
CLASSES = 8
NB = 256
LOG2E = math.log2(math.e)
NT = (((1,), (1,)), ((), ()))
TN = (((0,), (0,)), ((), ()))

OFFSETS = [(0, 0), (1, 0), (3, 0), (2, 0), (0, 1), (0, 3), (0, 2)]
OFFSETS += [(1, 1), (1, 3), (3, 1), (3, 3), (1, 2), (3, 2), (2, 1), (2, 3), (2, 2)]
PLACE = {o: i for i, o in enumerate(OFFSETS)}
GROUPS = ((0, 7), (7, 11), (11, 16))
Q_OFFSETS = [(0, 0), (-2, 0), (2, 0), (-1, 0), (0, 1), (-2, 1), (2, 1), (-1, 1)]
Q_OFFSETS += [(1, 0), (4, 0), (-3, 0), (3, 0), (1, 1), (4, 1), (-3, 1), (3, 1)]
Q_PLACE = {o: i for i, o in enumerate(Q_OFFSETS)}
OWN_CORE = (0, 1, 2, 3, 8, 9, 10, 11)


def split2(value):
    high = value.astype(BF16)
    return high, (value - high.astype(F32)).astype(BF16)


def as_row(rows):
    return jnp.concatenate(rows, axis=1)


def lanes_of(slot):
    return slice(slot * ROWS, (slot + 1) * ROWS)


def kernel(
    q_own, c_own, mask_hbm, rc_hbm, cc_hbm, cot_hbm, dq_out, dc_out,
    mask_ref, rc_ref, cc_ref, cot_ref, aux,
    qg, cg, qt, e, m_ref, l_ref, pt, pc, ot, post, st_own, st_sib, st_all, st_end, aqt,
    dcf, zs_sib, zr_sib, zp, zs1, zr1, zs2, zr2, xs1, xr1, xs2, xr2,
    in_s, q_ss, q_rs, qf_ss, qf_rs, a_ss, a_rs, af_ss, af_rs, c_ss, c_rs, t_ss, t_rs, zb_ss, zb_rs,
    z1_ss, z1_rs, z2_ss, z2_rs, x1_ss, x1_rs, x2_ss, x2_rs,
):
    kk = LOG2E / math.sqrt(D)
    x = lax.axis_index("col")
    row = lax.axis_index("row")
    core = row % 2
    z = (row // 2) % NZ
    y = row // (2 * NZ)
    par = (x + y) % 2
    zpar = z % 2
    zsig = 1 - 2 * zpar

    def dev(dx, dy, dz, dcore):
        ny, nz, nc = (y + dy) % NY, (z + dz) % NZ, (core + dcore) % 2
        return ((ny * NZ + nz) * 2 + nc, (x + dx) % NX)

    sibling = dev(0, 0, 0, 1)
    pending = []

    def send(src, dst, ssem, rsem, to):
        copy = pltpu.make_async_remote_copy(
            src_ref=src, dst_ref=dst, send_sem=ssem, recv_sem=rsem, device_id=to, device_id_type=MESH
        )
        copy.start()
        pending.append(copy)

    def arrived(dst, ssem, rsem):
        pltpu.make_async_remote_copy(
            src_ref=dst, dst_ref=dst, send_sem=ssem, recv_sem=rsem, device_id=sibling, device_id_type=MESH
        ).wait_recv()

    barrier = pltpu.get_barrier_semaphore()
    peers = [dev(0, 0, d, 0) for d in (2, 6, 1, 7)]
    peers += [dev(d, 0, 0, 0) for d in (2, 1, 3)]
    peers += [dev(0, d, 0, 0) for d in (2, 1, 3)]
    peers += [sibling]
    for peer in peers:
        pl.semaphore_signal(barrier, inc=1, device_id=peer, device_id_type=MESH)
    loads = [
        pltpu.make_async_copy(src, dst, in_s.at[i])
        for i, (src, dst) in enumerate(
            (
                (cot_hbm, cot_ref), (mask_hbm, mask_ref), (rc_hbm, rc_ref), (cc_hbm, cc_ref),
                (q_own, qg.at[0]), (c_own, cg.at[0]),
            )
        )
    ]
    for load in loads:
        load.start()
    pl.semaphore_wait(barrier, len(peers))

    z_hops = (2, -2, 1, -1)
    for i, hop in enumerate(z_hops):
        send(q_own, qg.at[Q_PLACE[-hop, 0]], q_ss.at[i], q_rs.at[i], dev(0, 0, hop, 0))
    for o in OFFSETS[1:7]:
        back = PLACE[(-o[0]) % NX, (-o[1]) % NY]
        send(c_own, cg.at[back], c_ss.at[back], c_rs.at[back], dev(o[0], o[1], 0, 0))
    send(q_own, qg.at[Q_PLACE[0, 1]], qf_ss.at[7], qf_rs.at[7], sibling)
    for load in loads:
        load.wait()
    aux[0] = jnp.broadcast_to(cot_ref[pl.ds(x, 1), :], (8, ROWS))
    for i, hop in enumerate(z_hops):
        send(aux.at[0], aux.at[Q_PLACE[-hop, 0]], a_ss.at[i], a_rs.at[i], dev(0, 0, hop, 0))
    send(aux.at[0], aux.at[Q_PLACE[0, 1]], af_ss.at[7], af_rs.at[7], sibling)

    lane256 = lax.broadcasted_iota(jnp.int32, (SLOTS, NB), 1)
    slot256 = lax.broadcasted_iota(jnp.int32, (SLOTS, NB), 0)
    q_block = jnp.zeros((SLOTS, NB), jnp.int32)
    for s, (dz, dc) in enumerate(Q_OFFSETS):
        block = ((y * NZ + (z + dz) % NZ) * 2 + (core + dc) % 2) * NX + x
        q_block = jnp.where(slot256 == s, block, q_block)
    sel_q = jnp.where(lane256 == q_block, 1.0, 0.0).astype(BF16)
    c_block = jnp.zeros((SLOTS, NB), jnp.int32)
    for b, (dx, dy) in enumerate(OFFSETS):
        block = ((((y + dy) % NY) * NZ + z) * 2 + core) * NX + (x + dx) % NX
        c_block = jnp.where(slot256 == b, block, c_block)
    sel_c = jnp.where(lane256 == c_block, 1.0, 0.0).astype(BF16)
    mask = mask_ref[...].astype(F32).astype(BF16)
    rc_all = rc_ref[...].astype(F32).astype(BF16)
    cc_all = cc_ref[...].astype(F32)
    m_sel = jnp.dot(sel_q, mask, preferred_element_type=F32).astype(BF16)
    rc = jnp.dot(sel_q, rc_all, preferred_element_type=F32)
    cc = jnp.dot(sel_c, cc_all.astype(BF16), preferred_element_type=F32)
    lane128 = lax.broadcasted_iota(jnp.int32, (ROWS, ROWS), 1)
    hist = jnp.zeros((NB, ROWS), F32)
    for k in range(CLASSES):
        column = jnp.where(lane128 == k, 1.0, 0.0).astype(BF16)
        same = jnp.where(cc_all == float(k), 1.0, 0.0).astype(BF16)
        hist = hist + jnp.dot(same, column, preferred_element_type=F32)
    per_class = jnp.dot(m_sel, hist.astype(BF16), preferred_element_type=F32)
    count = jnp.zeros((SLOTS, ROWS), F32)
    for k in range(CLASSES):
        count = jnp.where(rc == float(k), per_class[:, k : k + 1], count)
    per_count = 1.0 / jnp.maximum(count, 1.0)
    class_of = (lax.broadcasted_iota(jnp.int32, (ROWS, ROWS), 0) % CLASSES).astype(F32)
    slot_of = lax.broadcasted_iota(jnp.int32, (ROWS, ROWS), 0) // CLASSES

    def repeated(value):
        return jnp.broadcast_to(value[:, None, :], (SLOTS, CLASSES, NB)).reshape(ROWS, NB)

    sel_c_rows = repeated(sel_c.astype(F32)).astype(BF16)
    m_sel_rows = repeated(m_sel.astype(F32)).astype(BF16)
    hit_q = lax.dot_general(sel_c_rows, m_sel, NT, preferred_element_type=F32)
    hit_c = lax.dot_general(m_sel_rows, sel_c, NT, preferred_element_type=F32)
    for s in range(SLOTS):
        picked = jnp.where(rc[s : s + 1, :] == class_of, hit_q[:, s : s + 1], 0.0).astype(BF16)
        pt[0:ROWS, lanes_of(s)] = picked
        pt[ROWS:NB, lanes_of(s)] = picked
        picked = jnp.where(cc[s : s + 1, :] == class_of, hit_c[:, s : s + 1], 0.0).T.astype(BF16)
        pc[lanes_of(s), 0:ROWS] = picked
        pc[lanes_of(s), ROWS:NB] = picked

    def c_slot(even, odd):
        return even + par * (odd - even)

    turn = [
        (c_slot(4, 1), 1 - par, par, [((d, 0), (0, d)) for d in (1, 3, 2)], ((0, 1), (1, 0))),
        (c_slot(5, 2), 1 - par, par, [((d, 0), (0, d)) for d in (1, 3, 2)], ((0, 3), (3, 0))),
        (c_slot(3, 6), par, 1 - par, [((0, d), (d, 0)) for d in (1, 3, 2)], ((2, 0), (0, 2))),
    ]
    forwards = [0]

    def c_forward(slot, fx, fy, hops, origin):
        arrived(cg.at[slot], c_ss.at[slot], c_rs.at[slot])
        for even, odd in hops:
            d = max(even)
            there = [
                PLACE[((o[0] - h[0]) % NX, (o[1] - h[1]) % NY)] for o, h in zip(origin, (even, odd))
            ]
            there = c_slot(*there)
            i = 7 + forwards[0]
            send(cg.at[slot], cg.at[there], c_ss.at[i], c_rs.at[there], dev(fx * d, fy * d, 0, 0))
            forwards[0] += 1

    def q_arrived(i, dz):
        slot = Q_PLACE[dz, 0]
        arrived(qg.at[slot], q_ss.at[i], q_rs.at[i])

    def q_pass(i, dz):
        here, there = Q_PLACE[dz, 0], Q_PLACE[dz, 1]
        send(qg.at[here], qg.at[there], qf_ss.at[i], qf_rs.at[i], sibling)

    def a_pass(i, dz):
        here, there = Q_PLACE[dz, 0], Q_PLACE[dz, 1]
        arrived(aux.at[here], a_ss.at[i], a_rs.at[i])
        send(aux.at[here], aux.at[there], af_ss.at[i], af_rs.at[i], sibling)

    def onward(ref, ss, rs):
        far = Q_PLACE[-2, 0] + zpar * (Q_PLACE[2, 0] - Q_PLACE[-2, 0])
        send(ref.at[far], ref.at[Q_PLACE[4, 0]], ss.at[4], rs.at[4], dev(0, 0, 2 * zsig, 0))
        send(ref.at[Q_PLACE[-2, 0]], ref.at[Q_PLACE[-3, 0]], ss.at[5], rs.at[5], dev(0, 0, 1, 0))
        send(ref.at[Q_PLACE[2, 0]], ref.at[Q_PLACE[3, 0]], ss.at[6], rs.at[6], dev(0, 0, -1, 0))

    c_forward(*turn[0])
    c_forward(*turn[1])
    q_arrived(0, -2)
    q_arrived(1, 2)
    onward(qg, q_ss, q_rs)
    c_forward(*turn[2])
    q_pass(0, -2)
    q_pass(1, 2)
    q_arrived(2, -1)
    q_pass(2, -1)
    q_arrived(3, 1)
    q_pass(3, 1)
    a_pass(0, -2)
    a_pass(1, 2)
    a_pass(2, -1)
    a_pass(3, 1)
    onward(aux, a_ss, a_rs)
    for slot in (c_slot(1, 4), c_slot(2, 5), c_slot(6, 3)):
        arrived(cg.at[slot], c_ss.at[slot], c_rs.at[slot])

    def wave(g, q_first, q_last):
        first, last = GROUPS[g]
        rows = slice(first * ROWS, last * ROWS)
        lanes = slice(q_first * ROWS, q_last * ROWS)
        c_rows = cg[first:last].reshape((last - first) * ROWS, D)
        q_rows = qg[q_first:q_last].reshape((q_last - q_first) * ROWS, D)
        scores = lax.dot_general(c_rows, q_rows, NT, preferred_element_type=F32)
        top = jnp.max(scores, axis=0, keepdims=True)
        grown = jnp.exp2((scores - top) * kk)
        m_ref[g : g + 1, lanes] = top * kk
        l_ref[g : g + 1, lanes] = jnp.sum(grown, axis=0, keepdims=True)
        e[rows, lanes] = grown.astype(BF16)

    def c_wait(g):
        for slot in range(*GROUPS[g]):
            arrived(cg.at[slot], c_ss.at[slot], c_rs.at[slot])

    wave(0, 0, 4)
    for i, dz in ((7, 0), (0, -2), (1, 2), (2, -1)):
        slot = Q_PLACE[dz, 1]
        arrived(qg.at[slot], qf_ss.at[i], qf_rs.at[i])
    wave(0, 4, 8)
    c_wait(1)
    wave(1, 0, 8)
    for i, dz in ((5, -3), (6, 3), (4, 4)):
        q_arrived(i, dz)
        q_pass(i, dz)
    wave(0, 8, 12)
    wave(1, 8, 12)
    for i, dz in ((4, 4), (5, -3), (6, 3)):
        a_pass(i, dz)
    c_wait(2)
    wave(2, 0, 12)
    for i, dz in ((3, 1), (5, -3), (6, 3), (4, 4)):
        slot = Q_PLACE[dz, 1]
        arrived(qg.at[slot], qf_ss.at[i], qf_rs.at[i])
    for g in range(3):
        wave(g, 12, 16)
    tops = m_ref[0:3, :]
    top_tile = jnp.max(tops, axis=0, keepdims=True)
    mass = jnp.sum(l_ref[0:3, :] * jnp.exp2(tops - top_tile), axis=0, keepdims=True)
    log_tile = top_tile + jnp.log2(mass)

    places = [2 * ((z + dz) % NZ) + (core + dc) % 2 for dz, dc in Q_OFFSETS]

    def slot_rows(ref):
        return as_row([ref[pl.ds(place, 1), :] for place in places])

    for s, place in enumerate(places):
        st_own[pl.ds(place, 1), :] = log_tile[:, lanes_of(s)]
    send(st_own, st_sib, t_ss.at[0], t_rs.at[0], sibling)
    for s in range(SLOTS):
        qt[:, lanes_of(s)] = qg[s].T
    arrived(st_sib, t_ss.at[0], t_rs.at[0])
    log_a, log_b = st_own[...], st_sib[...]
    top = jnp.maximum(log_a, log_b)
    st_all[z] = top + jnp.log2(jnp.exp2(log_a - top) + jnp.exp2(log_b - top))
    for d in (4, 3, 5, 2, 6, 1, 7):
        send(st_all.at[z], st_all.at[z], t_ss.at[d], t_rs.at[d], dev(0, 0, d, 0))

    log_pair = slot_rows(st_all.at[z])
    shrink = jnp.exp2(tops - log_pair)
    own_class = [
        jnp.where((cc[b : b + 1, :] == class_of) & (slot_of == b), 1.0, 0.0).astype(BF16) for b in range(SLOTS)
    ]
    sums = jnp.dot(
        jnp.concatenate(own_class, axis=1), cg[...].reshape(TILE, D), preferred_element_type=F32
    )
    sums = jnp.concatenate(split2(sums), axis=0)

    def c_times_e(first):
        lanes = slice(first * ROWS, (first + 4) * ROWS)
        total = None
        for g, (start, stop) in enumerate(GROUPS):
            c_rows = cg[start:stop].reshape((stop - start) * ROWS, D)
            part = lax.dot_general(
                c_rows, e[start * ROWS : stop * ROWS, lanes], TN, preferred_element_type=F32
            )
            part = part * shrink[g : g + 1, lanes]
            total = part if total is None else total + part
        hits = lax.dot_general(sums, pt[:, lanes], TN, preferred_element_type=F32)
        return total, hits

    for half, first in enumerate((4, 12)):
        total, hits = c_times_e(first)
        for s in range(4):
            zs_sib[half, s, 0:D, :] = total[:, lanes_of(s)].astype(BF16)
            zs_sib[half, s, D : 2 * D, :] = hits[:, lanes_of(s)].astype(BF16)
        send(zs_sib.at[half], zr_sib.at[half], zb_ss.at[half], zb_rs.at[half], sibling)
    for half, first in enumerate((0, 8)):
        total, hits = c_times_e(first)
        for s in range(4):
            ot[4 * half + s] = total[:, lanes_of(s)]
            post[4 * half + s] = hits[:, lanes_of(s)]

    for i, dz in ((7, 0), (0, -2), (1, 2), (2, -1), (3, 1), (4, 4), (5, -3), (6, 3)):
        slot = Q_PLACE[dz, 1]
        arrived(aux.at[slot], af_ss.at[i], af_rs.at[i])
    cot = jnp.concatenate([aux[s, 0:1, :] for s in range(SLOTS)], axis=0)
    coef_pos = cot * per_count
    weights = [
        jnp.where((rc[s : s + 1, :] == class_of) & (slot_of == s), -coef_pos[s : s + 1, :], 0.0)
        for s in range(SLOTS)
    ]
    weights = jnp.concatenate(split2(jnp.concatenate(weights, axis=1)), axis=0)
    sums_q = jnp.dot(weights, qg[...].reshape(TILE, D), preferred_element_type=F32)
    sums_q = sums_q[0:ROWS, :] + sums_q[ROWS:NB, :]
    sums_q = jnp.concatenate(split2(sums_q), axis=0)
    soft_row = as_row([(count * per_count)[s : s + 1, :] for s in range(SLOTS)])
    cot_row = as_row([cot[s : s + 1, :] for s in range(SLOTS)])

    for d in (1, 7, 2, 6, 3, 5, 4):
        slot = (z - d + NZ) % NZ
        arrived(st_all.at[slot], t_ss.at[d], t_rs.at[d])
    top = st_all[0]
    for s in range(1, NZ):
        top = jnp.maximum(top, st_all[s])
    mass = jnp.zeros((SLOTS, ROWS), F32)
    for s in range(NZ):
        mass = mass + jnp.exp2(st_all[s] - top)
    st_end[0] = top
    st_end[1] = 1.0 / mass
    top_row = slot_rows(st_end.at[0])
    soft_row = soft_row * slot_rows(st_end.at[1])
    a_groups = soft_row * cot_row * jnp.exp2(tops - top_row)
    a_pair = soft_row * jnp.exp2(log_pair - top_row)

    def z_part(dz):
        return OWN_CORE.index(Q_PLACE[dz, 0])

    def z_sum(i):
        s = OWN_CORE[i]
        half, j = i // 4, i % 4
        soft = ot[i] + zr_sib[half, j, 0:D, :].astype(F32)
        hits = post[i] + zr_sib[half, j, D : 2 * D, :].astype(F32)
        return soft * a_pair[:, lanes_of(s)] - hits * per_count[s : s + 1, :]

    for half in range(2):
        arrived(zr_sib.at[half], zb_ss.at[half], zb_rs.at[half])
    for i, (target, hop) in enumerate(((4, -2 * zsig), (-3, -1), (3, 1))):
        zs1[i] = z_sum(z_part(target)).astype(BF16)
        send(zs1.at[i], zr1.at[i], z1_ss.at[i], z1_rs.at[i], dev(0, 0, hop, 0))

    def dc_group(g):
        first, last = GROUPS[g]
        rows = slice(first * ROWS, last * ROWS)
        aqt[g % 2] = (qt[...].astype(F32) * a_groups[g : g + 1, :]).astype(BF16)
        part = lax.dot_general(e[rows, :], aqt[g % 2], NT, preferred_element_type=F32)
        part = part + jnp.dot(pc[rows, :], sums_q, preferred_element_type=F32)
        dcf[first:last] = part.reshape(last - first, ROWS, D)

    def dc_send(slot, dx, dy):
        i = slot - 7
        xs1[i] = dcf[slot].astype(BF16)
        send(xs1.at[i], xr1.at[i], x1_ss.at[i], x1_rs.at[i], dev(dx, dy, 0, 0))

    def dc_hub(o, *others):
        total = dcf[PLACE[o]]
        for other in others:
            total = total + xr1[PLACE[other] - 7].astype(F32)
        if o in ((2, 0), (0, 2)):
            total = total + jnp.where(par == o[0] // 2, xr1[PLACE[2, 2] - 7].astype(F32), 0.0)
        i = PLACE[o] - 1
        xs2[i] = total.astype(BF16)
        send(xs2.at[i], xr2.at[i], x2_ss.at[i], x2_rs.at[i], dev(o[0], o[1], 0, 0))

    def dc_wait(*slots):
        for o in slots:
            i = PLACE[o] - 7
            arrived(xr1.at[i], x1_ss.at[i], x1_rs.at[i])

    dc_group(2)
    dc_send(PLACE[2, 2], 2 - 2 * par, 2 * par)
    for o, hop in (((1, 2), (1, 0)), ((2, 1), (0, 1)), ((3, 2), (3, 0)), ((2, 3), (0, 3))):
        dc_send(PLACE[o], *hop)
    for i, target in ((2, -1), (3, 1)):
        zs2[i] = z_sum(z_part(target)).astype(BF16)
        send(zs2.at[i], zr2.at[i], z2_ss.at[i], z2_rs.at[i], dev(0, 0, target, 0))
    dc_group(1)
    for o, hop in (((1, 1), (1, 0)), ((3, 1), (0, 1)), ((3, 3), (3, 0)), ((1, 3), (0, 3))):
        dc_send(PLACE[o], *hop)
    for target in (0, -2, 2):
        zp[z_part(target)] = z_sum(z_part(target))
    dc_group(0)
    for i in range(3):
        arrived(zr1.at[i], z1_ss.at[i], z1_rs.at[i])
    far = zr1[0].astype(F32)
    down = zp[z_part(-2)] + zr1[1].astype(F32) + jnp.where(zpar == 0, far, 0.0)
    up = zp[z_part(2)] + zr1[2].astype(F32) + jnp.where(zpar == 1, far, 0.0)
    zs2[0] = down.astype(BF16)
    zs2[1] = up.astype(BF16)
    send(zs2.at[0], zr2.at[0], z2_ss.at[0], z2_rs.at[0], dev(0, 0, -2, 0))
    send(zs2.at[1], zr2.at[1], z2_ss.at[1], z2_rs.at[1], dev(0, 0, 2, 0))

    dc_wait((2, 2), (2, 1), (2, 3))
    dc_hub((2, 0), (2, 1), (2, 3))
    dc_wait((1, 2), (3, 2))
    dc_hub((0, 2), (1, 2), (3, 2))
    for o, other in (((0, 1), (1, 1)), ((1, 0), (1, 3)), ((0, 3), (3, 3)), ((3, 0), (3, 1))):
        dc_wait(other)
        dc_hub(o, other)

    total = zp[0]
    for i in (2, 3, 0, 1):
        arrived(zr2.at[i], z2_ss.at[i], z2_rs.at[i])
        total = total + zr2[i].astype(F32)
    dq_out[...] = (total * cot[0:1, :]).T
    total = dcf[0]
    for i in range(6):
        arrived(xr2.at[i], x2_ss.at[i], x2_rs.at[i])
        total = total + xr2[i].astype(F32)
    dc_out[...] = total
    for copy in pending:
        copy.wait_send()


def shards(queries, candidates, block_mask, row_class, col_class, cotangent):
    dma = pltpu.SemaphoreType.DMA
    vmem = pltpu.VMEM
    block = (D, ROWS)
    scratch = [
        vmem((NB, NB), jnp.int32),
        vmem((NB, ROWS), jnp.int32),
        vmem((NB, ROWS), jnp.int32),
        vmem((NX, ROWS), F32),
        vmem((SLOTS, 8, ROWS), F32),
        vmem((SLOTS, ROWS, D), BF16),
        vmem((SLOTS, ROWS, D), BF16),
        vmem((D, TILE), BF16),
        vmem((TILE, TILE), BF16),
        vmem((8, TILE), F32),
        vmem((8, TILE), F32),
        vmem((NB, TILE), BF16),
        vmem((TILE, NB), BF16),
        vmem((8,) + block, F32),
        vmem((8,) + block, F32),
        vmem((SLOTS, ROWS), F32),
        vmem((SLOTS, ROWS), F32),
        vmem((NZ, SLOTS, ROWS), F32),
        vmem((2, SLOTS, ROWS), F32),
        vmem((2, D, TILE), BF16),
        vmem((SLOTS, ROWS, D), F32),
        vmem((2, 4, 2 * D, ROWS), BF16),
        vmem((2, 4, 2 * D, ROWS), BF16),
        vmem((8,) + block, F32),
        vmem((3,) + block, BF16),
        vmem((3,) + block, BF16),
        vmem((4,) + block, BF16),
        vmem((4,) + block, BF16),
        vmem((9, ROWS, D), BF16),
        vmem((9, ROWS, D), BF16),
        vmem((6, ROWS, D), BF16),
        vmem((6, ROWS, D), BF16),
        dma((6,)),
        dma((7,)), dma((7,)), dma((8,)), dma((8,)), dma((7,)), dma((7,)), dma((8,)), dma((8,)),
        dma((16,)), dma((16,)), dma((8,)), dma((8,)), dma((2,)), dma((2,)),
        dma((3,)), dma((3,)), dma((4,)), dma((4,)), dma((9,)), dma((9,)), dma((6,)), dma((6,)),
    ]
    out = vmem((ROWS, D), F32)
    dq, dc = pl.pallas_call(
        kernel,
        out_shape=(out, out),
        in_specs=[pl.BlockSpec(memory_space=pl.ANY)] * 6,
        out_specs=(pl.BlockSpec(memory_space=vmem), pl.BlockSpec(memory_space=vmem)),
        scratch_shapes=scratch,
        compiler_params=pltpu.CompilerParams(
            collective_id=0, has_side_effects=True, vmem_limit_bytes=56 * 2**20
        ),
    )(
        queries,
        candidates,
        block_mask,
        row_class.reshape(NB, ROWS),
        col_class.reshape(NB, ROWS),
        cotangent.reshape(NX, ROWS),
    )
    scale = 1.0 / math.sqrt(D)
    return dq * scale, dc * scale


def solution(mesh):
    in_specs = (P(("row", "col"), None), P(("row", "col"), None), P(), P(), P(), P("row"))
    out_specs = (P(("row", "col"), None), P(("row", "col"), None))
    return jax.shard_map(shards, mesh=mesh, in_specs=in_specs, out_specs=out_specs, check_vma=False)
```

```python
import math

import jax
import jax.numpy as jnp
from jax import lax
from jax.experimental import pallas as pl
from jax.experimental.pallas import tpu as pltpu
from jax.sharding import PartitionSpec as P

MESH = pl.DeviceIdType.MESH
F32 = jnp.float32
BF16 = jnp.bfloat16
ROWS = 128
SENT = ROWS + 16
D = 256
NX, NY, NZ = 4, 4, 8
TILE = 2048
SLOTS = 16
CLASSES = 8
NB = 256
LOG2E = math.log2(math.e)
NT = (((1,), (1,)), ((), ()))
TN = (((0,), (0,)), ((), ()))

OFFSETS = [(0, 0), (1, 0), (3, 0), (2, 0), (0, 1), (0, 3), (0, 2)]
OFFSETS += [(1, 1), (1, 3), (3, 1), (3, 3), (1, 2), (3, 2), (2, 1), (2, 3), (2, 2)]
PLACE = {o: i for i, o in enumerate(OFFSETS)}
GROUPS = ((0, 7), (7, 11), (11, 16))
Q_OFFSETS = [(0, 0), (-2, 0), (2, 0), (-1, 0), (0, 1), (-2, 1), (2, 1), (-1, 1)]
Q_OFFSETS += [(1, 0), (4, 0), (-3, 0), (3, 0), (1, 1), (4, 1), (-3, 1), (3, 1)]
Q_PLACE = {o: i for i, o in enumerate(Q_OFFSETS)}
OWN_CORE = (0, 1, 2, 3, 8, 9, 10, 11)


def split2(value):
    high = value.astype(BF16)
    return high, (value - high.astype(F32)).astype(BF16)


def as_row(rows):
    return jnp.concatenate(rows, axis=1)


def lanes_of(slot):
    return slice(slot * ROWS, (slot + 1) * ROWS)


def kernel(
    q_own, c_own, mask_hbm, rc_hbm, cc_hbm, cot_hbm, dq_out, dc_out,
    mask_ref, rc_ref, cc_ref, cot_ref,
    qg, cg, qt, e, m_ref, l_ref, pt, pc, ot, post, st_own, st_sib, st_all, st_end, aqt,
    dcf, zs_sib, zr_sib, zp, zs1, zr1, zs2, zr2, xs1, xr1, xs2, xr2,
    in_s, q_ss, q_rs, qf_ss, qf_rs, c_ss, c_rs, t_ss, t_rs, zb_ss, zb_rs,
    z1_ss, z1_rs, z2_ss, z2_rs, x1_ss, x1_rs, x2_ss, x2_rs,
):
    kk = LOG2E / math.sqrt(D)
    x = lax.axis_index("col")
    row = lax.axis_index("row")
    core = row % 2
    z = (row // 2) % NZ
    y = row // (2 * NZ)
    par = (x + y) % 2
    zpar = z % 2
    zsig = 1 - 2 * zpar

    def dev(dx, dy, dz, dcore):
        ny, nz, nc = (y + dy) % NY, (z + dz) % NZ, (core + dcore) % 2
        return ((ny * NZ + nz) * 2 + nc, (x + dx) % NX)

    sibling = dev(0, 0, 0, 1)
    pending = []

    def send(src, dst, ssem, rsem, to):
        copy = pltpu.make_async_remote_copy(
            src_ref=src, dst_ref=dst, send_sem=ssem, recv_sem=rsem, device_id=to, device_id_type=MESH
        )
        copy.start()
        pending.append(copy)

    def arrived(dst, ssem, rsem):
        pltpu.make_async_remote_copy(
            src_ref=dst, dst_ref=dst, send_sem=ssem, recv_sem=rsem, device_id=sibling, device_id_type=MESH
        ).wait_recv()

    barrier = pltpu.get_barrier_semaphore()
    peers = [dev(0, 0, d, 0) for d in (2, 6, 1, 7)]
    peers += [dev(d, 0, 0, 0) for d in (2, 1, 3)]
    peers += [dev(0, d, 0, 0) for d in (2, 1, 3)]
    peers += [sibling]
    for peer in peers:
        pl.semaphore_signal(barrier, inc=1, device_id=peer, device_id_type=MESH)
    loads = [
        pltpu.make_async_copy(src, dst, in_s.at[i])
        for i, (src, dst) in enumerate(
            (
                (q_own, qg.at[0, pl.ds(0, ROWS)]), (cot_hbm, cot_ref), (c_own, cg.at[0]),
                (mask_hbm, mask_ref), (rc_hbm, rc_ref), (cc_hbm, cc_ref),
            )
        )
    ]
    for load in loads:
        load.start()
    for load in loads[:3]:
        load.wait()
    own_cot = cot_ref[pl.ds(x, 1), :]
    high = own_cot.astype(BF16).astype(F32)
    middle = (own_cot - high).astype(BF16).astype(F32)
    low = own_cot - high - middle
    part_row = lax.broadcasted_iota(jnp.int32, (16, D), 0)
    parts = jnp.where(part_row == 0, jnp.concatenate([high, middle], axis=1), 0.0)
    parts = jnp.where(part_row == 1, jnp.concatenate([low, low], axis=1), parts)
    qg[0, ROWS:SENT, :] = parts.astype(BF16)
    pl.semaphore_wait(barrier, len(peers))

    z_hops = (2, -2, 1, -1)

    def q_first(i):
        hop = z_hops[i]
        send(qg.at[0], qg.at[Q_PLACE[-hop, 0]], q_ss.at[i], q_rs.at[i], dev(0, 0, hop, 0))

    def c_first(o):
        back = PLACE[(-o[0]) % NX, (-o[1]) % NY]
        send(cg.at[0], cg.at[back], c_ss.at[back], c_rs.at[back], dev(o[0], o[1], 0, 0))

    q_first(0)
    q_first(1)
    for o in ((2, 0), (0, 2), (1, 0), (0, 1), (3, 0), (0, 3)):
        c_first(o)
    q_first(2)
    q_first(3)
    for load in loads[3:]:
        load.wait()

    lane256 = lax.broadcasted_iota(jnp.int32, (SLOTS, NB), 1)
    slot256 = lax.broadcasted_iota(jnp.int32, (SLOTS, NB), 0)
    q_block = jnp.zeros((SLOTS, NB), jnp.int32)
    for s, (dz, dc) in enumerate(Q_OFFSETS):
        block = ((y * NZ + (z + dz) % NZ) * 2 + (core + dc) % 2) * NX + x
        q_block = jnp.where(slot256 == s, block, q_block)
    sel_q = jnp.where(lane256 == q_block, 1.0, 0.0).astype(BF16)
    c_block = jnp.zeros((SLOTS, NB), jnp.int32)
    for b, (dx, dy) in enumerate(OFFSETS):
        block = ((((y + dy) % NY) * NZ + z) * 2 + core) * NX + (x + dx) % NX
        c_block = jnp.where(slot256 == b, block, c_block)
    sel_c = jnp.where(lane256 == c_block, 1.0, 0.0).astype(BF16)
    mask = mask_ref[...].astype(F32).astype(BF16)
    rc_all = rc_ref[...].astype(F32).astype(BF16)
    cc_all = cc_ref[...].astype(F32)
    m_sel = jnp.dot(sel_q, mask, preferred_element_type=F32).astype(BF16)
    rc = jnp.dot(sel_q, rc_all, preferred_element_type=F32)
    cc = jnp.dot(sel_c, cc_all.astype(BF16), preferred_element_type=F32)
    lane128 = lax.broadcasted_iota(jnp.int32, (ROWS, ROWS), 1)
    hist = jnp.zeros((NB, ROWS), F32)
    for k in range(CLASSES):
        column = jnp.where(lane128 == k, 1.0, 0.0).astype(BF16)
        same = jnp.where(cc_all == float(k), 1.0, 0.0).astype(BF16)
        hist = hist + jnp.dot(same, column, preferred_element_type=F32)
    per_class = jnp.dot(m_sel, hist.astype(BF16), preferred_element_type=F32)
    count = jnp.zeros((SLOTS, ROWS), F32)
    for k in range(CLASSES):
        count = jnp.where(rc == float(k), per_class[:, k : k + 1], count)
    per_count = 1.0 / jnp.maximum(count, 1.0)
    class_of = (lax.broadcasted_iota(jnp.int32, (ROWS, ROWS), 0) % CLASSES).astype(F32)
    slot_of = lax.broadcasted_iota(jnp.int32, (ROWS, ROWS), 0) // CLASSES

    def repeated(value):
        return jnp.broadcast_to(value[:, None, :], (SLOTS, CLASSES, NB)).reshape(ROWS, NB)

    sel_c_rows = repeated(sel_c.astype(F32)).astype(BF16)
    m_sel_rows = repeated(m_sel.astype(F32)).astype(BF16)
    hit_q = lax.dot_general(sel_c_rows, m_sel, NT, preferred_element_type=F32)
    hit_c = lax.dot_general(m_sel_rows, sel_c, NT, preferred_element_type=F32)
    for s in range(SLOTS):
        picked = jnp.where(rc[s : s + 1, :] == class_of, hit_q[:, s : s + 1], 0.0).astype(BF16)
        pt[0:ROWS, lanes_of(s)] = picked
        pt[ROWS:NB, lanes_of(s)] = picked
        picked = jnp.where(cc[s : s + 1, :] == class_of, hit_c[:, s : s + 1], 0.0).T.astype(BF16)
        pc[lanes_of(s), 0:ROWS] = picked
        pc[lanes_of(s), ROWS:NB] = picked

    def c_here(*offsets):
        for o in offsets:
            arrived(cg.at[PLACE[o]], c_ss.at[PLACE[o]], c_rs.at[PLACE[o]])

    def c_forward(o, dx, dy):
        there = PLACE[(o[0] - dx) % NX, (o[1] - dy) % NY]
        send(cg.at[PLACE[o]], cg.at[there], c_ss.at[there], c_rs.at[there], dev(dx, dy, 0, 0))

    def q_arrived(i, dz):
        slot = Q_PLACE[dz, 0]
        arrived(qg.at[slot], q_ss.at[i], q_rs.at[i])

    def q_pass(i):
        here, there = qg.at[pl.ds(8 * i, 4)], qg.at[pl.ds(8 * i + 4, 4)]
        send(here, there, qf_ss.at[i], qf_rs.at[i], sibling)

    def q_passed(i):
        arrived(qg.at[pl.ds(8 * i + 4, 4)], qf_ss.at[i], qf_rs.at[i])

    q_far = Q_PLACE[-2, 0] + zpar * (Q_PLACE[2, 0] - Q_PLACE[-2, 0])
    onward = (
        (4, q_far, Q_PLACE[4, 0], 2 * zsig),
        (5, Q_PLACE[-2, 0], Q_PLACE[-3, 0], 1),
        (6, Q_PLACE[2, 0], Q_PLACE[3, 0], -1),
    )

    c_here((2, 0), (0, 2))
    for hop in (1, 3):
        c_forward((2, 0), 0, hop)
        c_forward((0, 2), hop, 0)
    q_arrived(0, -2)
    q_arrived(1, 2)
    for i, here, there, dz in onward:
        send(qg.at[here], qg.at[there], q_ss.at[i], q_rs.at[i], dev(0, 0, dz, 0))
    far = PLACE[2, 0] + par * (PLACE[0, 2] - PLACE[2, 0])
    there = PLACE[2, 2]
    send(cg.at[far], cg.at[there], c_ss.at[there], c_rs.at[there], dev(2 * par, 2 - 2 * par, 0, 0))
    for o, dx, dy in (((0, 1), 3, 0), ((0, 3), 1, 0), ((1, 0), 0, 1), ((3, 0), 0, 3)):
        c_here(o)
        c_forward(o, dx, dy)
    q_arrived(2, -1)
    q_pass(0)

    def wave(g, q_first, q_last):
        first, last = GROUPS[g]
        rows = slice(first * ROWS, last * ROWS)
        lanes = slice(q_first * ROWS, q_last * ROWS)
        c_rows = cg[first:last].reshape((last - first) * ROWS, D)
        q_rows = qg[q_first:q_last, 0:ROWS, :].reshape((q_last - q_first) * ROWS, D)
        scores = lax.dot_general(c_rows, q_rows, NT, preferred_element_type=F32)
        top = jnp.max(scores, axis=0, keepdims=True)
        grown = jnp.exp2((scores - top) * kk)
        m_ref[g : g + 1, lanes] = top * kk
        l_ref[g : g + 1, lanes] = jnp.sum(grown, axis=0, keepdims=True)
        e[rows, lanes] = grown.astype(BF16)

    def c_wait(g):
        for slot in range(*GROUPS[g]):
            arrived(cg.at[slot], c_ss.at[slot], c_rs.at[slot])

    wave(0, 0, 4)
    q_passed(0)
    wave(0, 4, 8)
    c_wait(1)
    wave(1, 0, 8)
    for i, dz in ((3, 1), (5, -3), (6, 3), (4, 4)):
        q_arrived(i, dz)
    q_pass(1)
    wave(0, 8, 12)
    wave(1, 8, 12)
    c_wait(2)
    wave(2, 0, 12)
    q_passed(1)
    for g in range(3):
        wave(g, 12, 16)
    tops = m_ref[0:3, :]
    top_tile = jnp.max(tops, axis=0, keepdims=True)
    mass = jnp.sum(l_ref[0:3, :] * jnp.exp2(tops - top_tile), axis=0, keepdims=True)
    log_tile = top_tile + jnp.log2(mass)

    places = [2 * ((z + dz) % NZ) + (core + dc) % 2 for dz, dc in Q_OFFSETS]

    def slot_rows(ref):
        return as_row([ref[pl.ds(place, 1), :] for place in places])

    for s, place in enumerate(places):
        st_own[pl.ds(place, 1), :] = log_tile[:, lanes_of(s)]
    send(st_own, st_sib, t_ss.at[0], t_rs.at[0], sibling)
    for s in range(SLOTS):
        qt[:, lanes_of(s)] = qg[s, 0:ROWS, :].T
    arrived(st_sib, t_ss.at[0], t_rs.at[0])
    log_a, log_b = st_own[...], st_sib[...]
    top = jnp.maximum(log_a, log_b)
    st_all[z] = top + jnp.log2(jnp.exp2(log_a - top) + jnp.exp2(log_b - top))
    for d in (4, 3, 5, 2, 6, 1, 7):
        send(st_all.at[z], st_all.at[z], t_ss.at[d], t_rs.at[d], dev(0, 0, d, 0))

    log_pair = slot_rows(st_all.at[z])
    shrink = jnp.exp2(tops - log_pair)
    own_class = [
        jnp.where((cc[b : b + 1, :] == class_of) & (slot_of == b), 1.0, 0.0).astype(BF16) for b in range(SLOTS)
    ]
    sums = jnp.dot(
        jnp.concatenate(own_class, axis=1), cg[...].reshape(TILE, D), preferred_element_type=F32
    )
    sums = jnp.concatenate(split2(sums), axis=0)

    def c_times_e(first):
        lanes = slice(first * ROWS, (first + 4) * ROWS)
        total = None
        for g, (start, stop) in enumerate(GROUPS):
            c_rows = cg[start:stop].reshape((stop - start) * ROWS, D)
            part = lax.dot_general(
                c_rows, e[start * ROWS : stop * ROWS, lanes], TN, preferred_element_type=F32
            )
            part = part * shrink[g : g + 1, lanes]
            total = part if total is None else total + part
        hits = lax.dot_general(sums, pt[:, lanes], TN, preferred_element_type=F32)
        return total, hits

    for half, first in enumerate((4, 12)):
        total, hits = c_times_e(first)
        for s in range(4):
            zs_sib[half, s, 0:D, :] = total[:, lanes_of(s)].astype(BF16)
            zs_sib[half, s, D : 2 * D, :] = hits[:, lanes_of(s)].astype(BF16)
        send(zs_sib.at[half], zr_sib.at[half], zb_ss.at[half], zb_rs.at[half], sibling)
    for half, first in enumerate((0, 8)):
        total, hits = c_times_e(first)
        for s in range(4):
            ot[4 * half + s] = total[:, lanes_of(s)]
            post[4 * half + s] = hits[:, lanes_of(s)]

    cot = []
    for s in range(SLOTS):
        parts = qg[s, ROWS:SENT, :].astype(F32)
        cot.append(parts[0:1, 0:ROWS] + parts[0:1, ROWS:D] + parts[1:2, 0:ROWS])
    cot = jnp.concatenate(cot, axis=0)
    coef_pos = cot * per_count
    weights = [
        jnp.where((rc[s : s + 1, :] == class_of) & (slot_of == s), -coef_pos[s : s + 1, :], 0.0)
        for s in range(SLOTS)
    ]
    weights = jnp.concatenate(split2(jnp.concatenate(weights, axis=1)), axis=0)
    sums_q = jnp.dot(weights, qg[:, 0:ROWS, :].reshape(TILE, D), preferred_element_type=F32)
    sums_q = sums_q[0:ROWS, :] + sums_q[ROWS:NB, :]
    sums_q = jnp.concatenate(split2(sums_q), axis=0)
    soft_row = as_row([(count * per_count)[s : s + 1, :] for s in range(SLOTS)])
    cot_row = as_row([cot[s : s + 1, :] for s in range(SLOTS)])

    for d in (1, 7, 2, 6, 3, 5, 4):
        slot = (z - d + NZ) % NZ
        arrived(st_all.at[slot], t_ss.at[d], t_rs.at[d])
    top = st_all[0]
    for s in range(1, NZ):
        top = jnp.maximum(top, st_all[s])
    mass = jnp.zeros((SLOTS, ROWS), F32)
    for s in range(NZ):
        mass = mass + jnp.exp2(st_all[s] - top)
    st_end[0] = top
    st_end[1] = 1.0 / mass
    top_row = slot_rows(st_end.at[0])
    soft_row = soft_row * slot_rows(st_end.at[1])
    a_groups = soft_row * cot_row * jnp.exp2(tops - top_row)
    a_pair = soft_row * jnp.exp2(log_pair - top_row)

    def z_part(dz):
        return OWN_CORE.index(Q_PLACE[dz, 0])

    def z_sum(i):
        s = OWN_CORE[i]
        half, j = i // 4, i % 4
        soft = ot[i] + zr_sib[half, j, 0:D, :].astype(F32)
        hits = post[i] + zr_sib[half, j, D : 2 * D, :].astype(F32)
        return soft * a_pair[:, lanes_of(s)] - hits * per_count[s : s + 1, :]

    for half in range(2):
        arrived(zr_sib.at[half], zb_ss.at[half], zb_rs.at[half])

    def dc_group(g):
        first, last = GROUPS[g]
        rows = slice(first * ROWS, last * ROWS)
        aqt[g % 2] = (qt[...].astype(F32) * a_groups[g : g + 1, :]).astype(BF16)
        part = lax.dot_general(e[rows, :], aqt[g % 2], NT, preferred_element_type=F32)
        part = part + jnp.dot(pc[rows, :], sums_q, preferred_element_type=F32)
        dcf[first:last] = part.reshape(last - first, ROWS, D)

    def dc_send(slot, dx, dy):
        i = slot - 7
        xs1[i] = dcf[slot].astype(BF16)
        send(xs1.at[i], xr1.at[i], x1_ss.at[i], x1_rs.at[i], dev(dx, dy, 0, 0))

    def dc_hub(o, *others):
        total = dcf[PLACE[o]]
        for other in others:
            total = total + xr1[PLACE[other] - 7].astype(F32)
        if o in ((2, 0), (0, 2)):
            total = total + jnp.where(par == o[0] // 2, xr1[PLACE[2, 2] - 7].astype(F32), 0.0)
        i = PLACE[o] - 1
        xs2[i] = total.astype(BF16)
        send(xs2.at[i], xr2.at[i], x2_ss.at[i], x2_rs.at[i], dev(o[0], o[1], 0, 0))

    def dc_wait(*slots):
        for o in slots:
            i = PLACE[o] - 7
            arrived(xr1.at[i], x1_ss.at[i], x1_rs.at[i])

    for i, (target, hop) in enumerate(((4, -2 * zsig), (-3, -1), (3, 1))):
        zs1[i] = z_sum(z_part(target)).astype(BF16)
        send(zs1.at[i], zr1.at[i], z1_ss.at[i], z1_rs.at[i], dev(0, 0, hop, 0))
    dc_group(2)
    dc_send(PLACE[2, 2], 2 - 2 * par, 2 * par)
    for o, hop in (((1, 2), (1, 0)), ((2, 1), (0, 1)), ((3, 2), (3, 0)), ((2, 3), (0, 3))):
        dc_send(PLACE[o], *hop)
    for i, target in ((2, -1), (3, 1)):
        zs2[i] = z_sum(z_part(target)).astype(BF16)
        send(zs2.at[i], zr2.at[i], z2_ss.at[i], z2_rs.at[i], dev(0, 0, target, 0))
    dc_group(1)
    for o, hop in (((1, 1), (1, 0)), ((3, 1), (0, 1)), ((3, 3), (3, 0)), ((1, 3), (0, 3))):
        dc_send(PLACE[o], *hop)
    for target in (0, -2, 2):
        zp[z_part(target)] = z_sum(z_part(target))
    dc_group(0)
    for i in range(3):
        arrived(zr1.at[i], z1_ss.at[i], z1_rs.at[i])
    far = zr1[0].astype(F32)
    down = zp[z_part(-2)] + zr1[1].astype(F32) + jnp.where(zpar == 0, far, 0.0)
    up = zp[z_part(2)] + zr1[2].astype(F32) + jnp.where(zpar == 1, far, 0.0)
    zs2[0] = down.astype(BF16)
    zs2[1] = up.astype(BF16)
    send(zs2.at[0], zr2.at[0], z2_ss.at[0], z2_rs.at[0], dev(0, 0, -2, 0))
    send(zs2.at[1], zr2.at[1], z2_ss.at[1], z2_rs.at[1], dev(0, 0, 2, 0))

    dc_wait((2, 2), (2, 1), (2, 3))
    dc_hub((2, 0), (2, 1), (2, 3))
    dc_wait((1, 2), (3, 2))
    dc_hub((0, 2), (1, 2), (3, 2))
    for o, other in (((0, 1), (1, 1)), ((1, 0), (1, 3)), ((0, 3), (3, 3)), ((3, 0), (3, 1))):
        dc_wait(other)
        dc_hub(o, other)

    total = zp[0]
    for i in (2, 3, 0, 1):
        arrived(zr2.at[i], z2_ss.at[i], z2_rs.at[i])
        total = total + zr2[i].astype(F32)
    dq_out[...] = (total * cot[0:1, :]).T
    total = dcf[0]
    for i in range(6):
        arrived(xr2.at[i], x2_ss.at[i], x2_rs.at[i])
        total = total + xr2[i].astype(F32)
    dc_out[...] = total
    for copy in pending:
        copy.wait_send()


def shards(queries, candidates, block_mask, row_class, col_class, cotangent):
    dma = pltpu.SemaphoreType.DMA
    vmem = pltpu.VMEM
    block = (D, ROWS)
    scratch = [
        vmem((NB, NB), jnp.int32),
        vmem((NB, ROWS), jnp.int32),
        vmem((NB, ROWS), jnp.int32),
        vmem((NX, ROWS), F32),
        vmem((SLOTS, SENT, D), BF16),
        vmem((SLOTS, ROWS, D), BF16),
        vmem((D, TILE), BF16),
        vmem((TILE, TILE), BF16),
        vmem((8, TILE), F32),
        vmem((8, TILE), F32),
        vmem((NB, TILE), BF16),
        vmem((TILE, NB), BF16),
        vmem((8,) + block, F32),
        vmem((8,) + block, F32),
        vmem((SLOTS, ROWS), F32),
        vmem((SLOTS, ROWS), F32),
        vmem((NZ, SLOTS, ROWS), F32),
        vmem((2, SLOTS, ROWS), F32),
        vmem((2, D, TILE), BF16),
        vmem((SLOTS, ROWS, D), F32),
        vmem((2, 4, 2 * D, ROWS), BF16),
        vmem((2, 4, 2 * D, ROWS), BF16),
        vmem((8,) + block, F32),
        vmem((3,) + block, BF16),
        vmem((3,) + block, BF16),
        vmem((4,) + block, BF16),
        vmem((4,) + block, BF16),
        vmem((9, ROWS, D), BF16),
        vmem((9, ROWS, D), BF16),
        vmem((6, ROWS, D), BF16),
        vmem((6, ROWS, D), BF16),
        dma((6,)),
        dma((7,)), dma((7,)), dma((2,)), dma((2,)),
        dma((16,)), dma((16,)), dma((8,)), dma((8,)), dma((2,)), dma((2,)),
        dma((3,)), dma((3,)), dma((4,)), dma((4,)), dma((9,)), dma((9,)), dma((6,)), dma((6,)),
    ]
    out = vmem((ROWS, D), F32)
    dq, dc = pl.pallas_call(
        kernel,
        out_shape=(out, out),
        in_specs=[pl.BlockSpec(memory_space=pl.ANY)] * 6,
        out_specs=(pl.BlockSpec(memory_space=vmem), pl.BlockSpec(memory_space=vmem)),
        scratch_shapes=scratch,
        compiler_params=pltpu.CompilerParams(
            collective_id=0, has_side_effects=True, vmem_limit_bytes=56 * 2**20
        ),
    )(
        queries,
        candidates,
        block_mask,
        row_class.reshape(NB, ROWS),
        col_class.reshape(NB, ROWS),
        cotangent.reshape(NX, ROWS),
    )
    scale = 1.0 / math.sqrt(D)
    return dq * scale, dc * scale


def solution(mesh):
    in_specs = (P(("row", "col"), None), P(("row", "col"), None), P(), P(), P(), P("row"))
    out_specs = (P(("row", "col"), None), P(("row", "col"), None))
    return jax.shard_map(shards, mesh=mesh, in_specs=in_specs, out_specs=out_specs, check_vma=False)
```

```python
import math

import jax
import jax.numpy as jnp
from jax import lax
from jax.experimental import pallas as pl
from jax.experimental.pallas import tpu as pltpu
from jax.sharding import PartitionSpec as P

MESH = pl.DeviceIdType.MESH
F32 = jnp.float32
BF16 = jnp.bfloat16
ROWS = 128
SENT = ROWS + 16
D = 256
NX, NY, NZ = 4, 4, 8
TILE = 2048
SLOTS = 16
CLASSES = 8
NB = 256
LOG2E = math.log2(math.e)
NT = (((1,), (1,)), ((), ()))
TN = (((0,), (0,)), ((), ()))

OFFSETS = [(0, 0), (1, 0), (3, 0), (2, 0), (0, 1), (0, 3), (0, 2)]
OFFSETS += [(1, 1), (1, 3), (3, 1), (3, 3), (1, 2), (3, 2), (2, 1), (2, 3), (2, 2)]
PLACE = {o: i for i, o in enumerate(OFFSETS)}
GROUPS = ((0, 7), (7, 11), (11, 16))
Q_OFFSETS = [(0, 0), (-2, 0), (2, 0), (-1, 0), (0, 1), (-2, 1), (2, 1), (-1, 1)]
Q_OFFSETS += [(1, 0), (4, 0), (-3, 0), (3, 0), (1, 1), (4, 1), (-3, 1), (3, 1)]
Q_PLACE = {o: i for i, o in enumerate(Q_OFFSETS)}
OWN_CORE = (0, 1, 2, 3, 8, 9, 10, 11)


def split2(value):
    high = value.astype(BF16)
    return high, (value - high.astype(F32)).astype(BF16)


def as_row(rows):
    return jnp.concatenate(rows, axis=1)


def lanes_of(slot):
    return slice(slot * ROWS, (slot + 1) * ROWS)


def kernel(
    q_own, c_own, mask_hbm, rc_hbm, cc_hbm, cot_hbm, dq_out, dc_out,
    mask_ref, rc_ref, cc_ref, cot_ref,
    qg, cg, qt, e, m_ref, l_ref, pt, pc, ot, post, st_own, st_sib, st_all, st_end, aqt,
    dcf, zs_sib, zr_sib, zp, zs1, zr1, zs2, zr2, xs1, xr1, xs2, xr2,
    in_s, q_ss, q_rs, qf_ss, qf_rs, c_ss, c_rs, t_ss, t_rs, zb_ss, zb_rs,
    z1_ss, z1_rs, z2_ss, z2_rs, x1_ss, x1_rs, x2_ss, x2_rs,
):
    kk = LOG2E / math.sqrt(D)
    x = lax.axis_index("col")
    row = lax.axis_index("row")
    core = row % 2
    z = (row // 2) % NZ
    y = row // (2 * NZ)
    par = (x + y) % 2
    zpar = z % 2
    zsig = 1 - 2 * zpar

    def dev(dx, dy, dz, dcore):
        ny, nz, nc = (y + dy) % NY, (z + dz) % NZ, (core + dcore) % 2
        return ((ny * NZ + nz) * 2 + nc, (x + dx) % NX)

    sibling = dev(0, 0, 0, 1)
    pending = []

    def send(src, dst, ssem, rsem, to):
        copy = pltpu.make_async_remote_copy(
            src_ref=src, dst_ref=dst, send_sem=ssem, recv_sem=rsem, device_id=to, device_id_type=MESH
        )
        copy.start()
        pending.append(copy)

    def arrived(dst, ssem, rsem):
        pltpu.make_async_remote_copy(
            src_ref=dst, dst_ref=dst, send_sem=ssem, recv_sem=rsem, device_id=sibling, device_id_type=MESH
        ).wait_recv()

    barrier = pltpu.get_barrier_semaphore()
    peers = [dev(0, 0, d, 0) for d in (2, 6, 1, 7)]
    peers += [dev(d, 0, 0, 0) for d in (2, 1, 3)]
    peers += [dev(0, d, 0, 0) for d in (2, 1, 3)]
    peers += [sibling]
    for peer in peers:
        pl.semaphore_signal(barrier, inc=1, device_id=peer, device_id_type=MESH)
    loads = [
        pltpu.make_async_copy(src, dst, in_s.at[i])
        for i, (src, dst) in enumerate(
            (
                (q_own, qg.at[0, pl.ds(0, ROWS)]), (cot_hbm, cot_ref), (c_own, cg.at[0]),
                (mask_hbm, mask_ref), (rc_hbm, rc_ref), (cc_hbm, cc_ref),
            )
        )
    ]
    for load in loads:
        load.start()
    for load in loads[:3]:
        load.wait()
    own_cot = cot_ref[pl.ds(x, 1), :]
    high = own_cot.astype(BF16).astype(F32)
    middle = (own_cot - high).astype(BF16).astype(F32)
    low = own_cot - high - middle
    part_row = lax.broadcasted_iota(jnp.int32, (16, D), 0)
    parts = jnp.where(part_row == 0, jnp.concatenate([high, middle], axis=1), 0.0)
    parts = jnp.where(part_row == 1, jnp.concatenate([low, low], axis=1), parts)
    qg[0, ROWS:SENT, :] = parts.astype(BF16)
    pl.semaphore_wait(barrier, len(peers))

    z_hops = (2, -2, 1, -1)

    def q_first(i):
        hop = z_hops[i]
        send(qg.at[0], qg.at[Q_PLACE[-hop, 0]], q_ss.at[i], q_rs.at[i], dev(0, 0, hop, 0))

    def c_first(o):
        back = PLACE[(-o[0]) % NX, (-o[1]) % NY]
        send(cg.at[0], cg.at[back], c_ss.at[back], c_rs.at[back], dev(o[0], o[1], 0, 0))

    for i in range(4):
        q_first(i)
    for o in ((2, 0), (0, 2), (1, 0), (0, 1), (3, 0), (0, 3)):
        c_first(o)
    for load in loads[3:]:
        load.wait()

    lane256 = lax.broadcasted_iota(jnp.int32, (SLOTS, NB), 1)
    slot256 = lax.broadcasted_iota(jnp.int32, (SLOTS, NB), 0)
    q_block = jnp.zeros((SLOTS, NB), jnp.int32)
    for s, (dz, dc) in enumerate(Q_OFFSETS):
        block = ((y * NZ + (z + dz) % NZ) * 2 + (core + dc) % 2) * NX + x
        q_block = jnp.where(slot256 == s, block, q_block)
    sel_q = jnp.where(lane256 == q_block, 1.0, 0.0).astype(BF16)
    c_block = jnp.zeros((SLOTS, NB), jnp.int32)
    for b, (dx, dy) in enumerate(OFFSETS):
        block = ((((y + dy) % NY) * NZ + z) * 2 + core) * NX + (x + dx) % NX
        c_block = jnp.where(slot256 == b, block, c_block)
    sel_c = jnp.where(lane256 == c_block, 1.0, 0.0).astype(BF16)
    mask = mask_ref[...].astype(F32).astype(BF16)
    rc_all = rc_ref[...].astype(F32).astype(BF16)
    cc_all = cc_ref[...].astype(F32)
    m_sel = jnp.dot(sel_q, mask, preferred_element_type=F32).astype(BF16)
    rc = jnp.dot(sel_q, rc_all, preferred_element_type=F32)
    cc = jnp.dot(sel_c, cc_all.astype(BF16), preferred_element_type=F32)
    lane128 = lax.broadcasted_iota(jnp.int32, (ROWS, ROWS), 1)
    hist = jnp.zeros((NB, ROWS), F32)
    for k in range(CLASSES):
        column = jnp.where(lane128 == k, 1.0, 0.0).astype(BF16)
        same = jnp.where(cc_all == float(k), 1.0, 0.0).astype(BF16)
        hist = hist + jnp.dot(same, column, preferred_element_type=F32)
    per_class = jnp.dot(m_sel, hist.astype(BF16), preferred_element_type=F32)
    count = jnp.zeros((SLOTS, ROWS), F32)
    for k in range(CLASSES):
        count = jnp.where(rc == float(k), per_class[:, k : k + 1], count)
    per_count = 1.0 / jnp.maximum(count, 1.0)
    class_of = (lax.broadcasted_iota(jnp.int32, (ROWS, ROWS), 0) % CLASSES).astype(F32)
    slot_of = lax.broadcasted_iota(jnp.int32, (ROWS, ROWS), 0) // CLASSES

    def repeated(value):
        return jnp.broadcast_to(value[:, None, :], (SLOTS, CLASSES, NB)).reshape(ROWS, NB)

    sel_c_rows = repeated(sel_c.astype(F32)).astype(BF16)
    m_sel_rows = repeated(m_sel.astype(F32)).astype(BF16)
    hit_q = lax.dot_general(sel_c_rows, m_sel, NT, preferred_element_type=F32)
    hit_c = lax.dot_general(m_sel_rows, sel_c, NT, preferred_element_type=F32)
    for s in range(SLOTS):
        picked = jnp.where(rc[s : s + 1, :] == class_of, hit_q[:, s : s + 1], 0.0).astype(BF16)
        pt[0:ROWS, lanes_of(s)] = picked
        pt[ROWS:NB, lanes_of(s)] = picked
        picked = jnp.where(cc[s : s + 1, :] == class_of, hit_c[:, s : s + 1], 0.0).T.astype(BF16)
        pc[lanes_of(s), 0:ROWS] = picked
        pc[lanes_of(s), ROWS:NB] = picked

    def c_here(*offsets):
        for o in offsets:
            arrived(cg.at[PLACE[o]], c_ss.at[PLACE[o]], c_rs.at[PLACE[o]])

    def c_forward(o, dx, dy):
        there = PLACE[(o[0] - dx) % NX, (o[1] - dy) % NY]
        send(cg.at[PLACE[o]], cg.at[there], c_ss.at[there], c_rs.at[there], dev(dx, dy, 0, 0))

    def q_arrived(i, dz):
        slot = Q_PLACE[dz, 0]
        arrived(qg.at[slot], q_ss.at[i], q_rs.at[i])

    def q_pass(i):
        here, there = qg.at[pl.ds(8 * i, 4)], qg.at[pl.ds(8 * i + 4, 4)]
        send(here, there, qf_ss.at[i], qf_rs.at[i], sibling)

    def q_passed(i):
        arrived(qg.at[pl.ds(8 * i + 4, 4)], qf_ss.at[i], qf_rs.at[i])

    q_far = Q_PLACE[-2, 0] + zpar * (Q_PLACE[2, 0] - Q_PLACE[-2, 0])
    onward = (
        (4, q_far, Q_PLACE[4, 0], 2 * zsig),
        (5, Q_PLACE[-2, 0], Q_PLACE[-3, 0], 1),
        (6, Q_PLACE[2, 0], Q_PLACE[3, 0], -1),
    )

    c_here((2, 0), (0, 2))
    for hop in (1, 3):
        c_forward((2, 0), 0, hop)
        c_forward((0, 2), hop, 0)
    q_arrived(0, -2)
    q_arrived(1, 2)
    for i, here, there, dz in onward:
        send(qg.at[here], qg.at[there], q_ss.at[i], q_rs.at[i], dev(0, 0, dz, 0))
    far = PLACE[2, 0] + par * (PLACE[0, 2] - PLACE[2, 0])
    there = PLACE[2, 2]
    send(cg.at[far], cg.at[there], c_ss.at[there], c_rs.at[there], dev(2 * par, 2 - 2 * par, 0, 0))
    for o, dx, dy in (((0, 1), 3, 0), ((0, 3), 1, 0), ((1, 0), 0, 1), ((3, 0), 0, 3)):
        c_here(o)
        c_forward(o, dx, dy)
    q_arrived(2, -1)
    q_pass(0)

    def wave(g, q_first, q_last):
        first, last = GROUPS[g]
        rows = slice(first * ROWS, last * ROWS)
        lanes = slice(q_first * ROWS, q_last * ROWS)
        c_rows = cg[first:last].reshape((last - first) * ROWS, D)
        q_rows = qg[q_first:q_last, 0:ROWS, :].reshape((q_last - q_first) * ROWS, D)
        scores = lax.dot_general(c_rows, q_rows, NT, preferred_element_type=F32)
        top = jnp.max(scores, axis=0, keepdims=True)
        grown = jnp.exp2((scores - top) * kk)
        m_ref[g : g + 1, lanes] = top * kk
        l_ref[g : g + 1, lanes] = jnp.sum(grown, axis=0, keepdims=True)
        e[rows, lanes] = grown.astype(BF16)

    def c_wait(g):
        for slot in range(*GROUPS[g]):
            arrived(cg.at[slot], c_ss.at[slot], c_rs.at[slot])

    wave(0, 0, 4)
    q_passed(0)
    wave(0, 4, 8)
    c_wait(1)
    wave(1, 0, 8)
    for i, dz in ((3, 1), (5, -3), (6, 3), (4, 4)):
        q_arrived(i, dz)
    q_pass(1)
    c_wait(2)
    wave(2, 0, 8)
    for g in range(3):
        wave(g, 8, 12)
    q_passed(1)
    for g in range(3):
        wave(g, 12, 16)
    tops = m_ref[0:3, :]
    top_tile = jnp.max(tops, axis=0, keepdims=True)
    mass = jnp.sum(l_ref[0:3, :] * jnp.exp2(tops - top_tile), axis=0, keepdims=True)
    log_tile = top_tile + jnp.log2(mass)

    places = [2 * ((z + dz) % NZ) + (core + dc) % 2 for dz, dc in Q_OFFSETS]

    def slot_rows(ref):
        return as_row([ref[pl.ds(place, 1), :] for place in places])

    for s, place in enumerate(places):
        st_own[pl.ds(place, 1), :] = log_tile[:, lanes_of(s)]
    send(st_own, st_sib, t_ss.at[0], t_rs.at[0], sibling)
    for s in range(SLOTS):
        qt[:, lanes_of(s)] = qg[s, 0:ROWS, :].T
    arrived(st_sib, t_ss.at[0], t_rs.at[0])
    log_a, log_b = st_own[...], st_sib[...]
    top = jnp.maximum(log_a, log_b)
    st_all[z] = top + jnp.log2(jnp.exp2(log_a - top) + jnp.exp2(log_b - top))
    for d in (4, 3, 5, 2, 6, 1, 7):
        send(st_all.at[z], st_all.at[z], t_ss.at[d], t_rs.at[d], dev(0, 0, d, 0))

    log_pair = slot_rows(st_all.at[z])
    shrink = jnp.exp2(tops - log_pair)
    own_class = [
        jnp.where((cc[b : b + 1, :] == class_of) & (slot_of == b), 1.0, 0.0).astype(BF16) for b in range(SLOTS)
    ]
    sums = jnp.dot(
        jnp.concatenate(own_class, axis=1), cg[...].reshape(TILE, D), preferred_element_type=F32
    )
    sums = jnp.concatenate(split2(sums), axis=0)

    def c_times_e(first):
        lanes = slice(first * ROWS, (first + 4) * ROWS)
        total = None
        for g, (start, stop) in enumerate(GROUPS):
            c_rows = cg[start:stop].reshape((stop - start) * ROWS, D)
            part = lax.dot_general(
                c_rows, e[start * ROWS : stop * ROWS, lanes], TN, preferred_element_type=F32
            )
            part = part * shrink[g : g + 1, lanes]
            total = part if total is None else total + part
        hits = lax.dot_general(sums, pt[:, lanes], TN, preferred_element_type=F32)
        return total, hits

    for half, first in enumerate((4, 12)):
        total, hits = c_times_e(first)
        for s in range(4):
            zs_sib[half, s, 0:D, :] = total[:, lanes_of(s)].astype(BF16)
            zs_sib[half, s, D : 2 * D, :] = hits[:, lanes_of(s)].astype(BF16)
        send(zs_sib.at[half], zr_sib.at[half], zb_ss.at[half], zb_rs.at[half], sibling)
    for half, first in enumerate((0, 8)):
        total, hits = c_times_e(first)
        for s in range(4):
            ot[4 * half + s] = total[:, lanes_of(s)]
            post[4 * half + s] = hits[:, lanes_of(s)]

    cot = []
    for s in range(SLOTS):
        parts = qg[s, ROWS:SENT, :].astype(F32)
        cot.append(parts[0:1, 0:ROWS] + parts[0:1, ROWS:D] + parts[1:2, 0:ROWS])
    cot = jnp.concatenate(cot, axis=0)
    coef_pos = cot * per_count
    weights = [
        jnp.where((rc[s : s + 1, :] == class_of) & (slot_of == s), -coef_pos[s : s + 1, :], 0.0)
        for s in range(SLOTS)
    ]
    weights = jnp.concatenate(split2(jnp.concatenate(weights, axis=1)), axis=0)
    sums_q = jnp.dot(weights, qg[:, 0:ROWS, :].reshape(TILE, D), preferred_element_type=F32)
    sums_q = sums_q[0:ROWS, :] + sums_q[ROWS:NB, :]
    sums_q = jnp.concatenate(split2(sums_q), axis=0)
    soft_row = as_row([(count * per_count)[s : s + 1, :] for s in range(SLOTS)])
    cot_row = as_row([cot[s : s + 1, :] for s in range(SLOTS)])

    for d in (1, 7, 2, 6, 3, 5, 4):
        slot = (z - d + NZ) % NZ
        arrived(st_all.at[slot], t_ss.at[d], t_rs.at[d])
    top = st_all[0]
    for s in range(1, NZ):
        top = jnp.maximum(top, st_all[s])
    mass = jnp.zeros((SLOTS, ROWS), F32)
    for s in range(NZ):
        mass = mass + jnp.exp2(st_all[s] - top)
    st_end[0] = top
    st_end[1] = 1.0 / mass
    top_row = slot_rows(st_end.at[0])
    soft_row = soft_row * slot_rows(st_end.at[1])
    a_groups = soft_row * cot_row * jnp.exp2(tops - top_row)
    a_pair = soft_row * jnp.exp2(log_pair - top_row)

    def z_part(dz):
        return OWN_CORE.index(Q_PLACE[dz, 0])

    def z_sum(i):
        s = OWN_CORE[i]
        half, j = i // 4, i % 4
        soft = ot[i] + zr_sib[half, j, 0:D, :].astype(F32)
        hits = post[i] + zr_sib[half, j, D : 2 * D, :].astype(F32)
        return soft * a_pair[:, lanes_of(s)] - hits * per_count[s : s + 1, :]

    for half in range(2):
        arrived(zr_sib.at[half], zb_ss.at[half], zb_rs.at[half])

    def dc_group(g):
        first, last = GROUPS[g]
        rows = slice(first * ROWS, last * ROWS)
        aqt[g % 2] = (qt[...].astype(F32) * a_groups[g : g + 1, :]).astype(BF16)
        part = lax.dot_general(e[rows, :], aqt[g % 2], NT, preferred_element_type=F32)
        part = part + jnp.dot(pc[rows, :], sums_q, preferred_element_type=F32)
        dcf[first:last] = part.reshape(last - first, ROWS, D)

    def dc_send(slot, dx, dy):
        i = slot - 7
        xs1[i] = dcf[slot].astype(BF16)
        send(xs1.at[i], xr1.at[i], x1_ss.at[i], x1_rs.at[i], dev(dx, dy, 0, 0))

    def dc_hub(o, *others):
        total = dcf[PLACE[o]]
        for other in others:
            total = total + xr1[PLACE[other] - 7].astype(F32)
        if o in ((2, 0), (0, 2)):
            total = total + jnp.where(par == o[0] // 2, xr1[PLACE[2, 2] - 7].astype(F32), 0.0)
        i = PLACE[o] - 1
        xs2[i] = total.astype(BF16)
        send(xs2.at[i], xr2.at[i], x2_ss.at[i], x2_rs.at[i], dev(o[0], o[1], 0, 0))

    def dc_wait(*slots):
        for o in slots:
            i = PLACE[o] - 7
            arrived(xr1.at[i], x1_ss.at[i], x1_rs.at[i])

    for i, (target, hop) in enumerate(((4, -2 * zsig), (-3, -1), (3, 1))):
        zs1[i] = z_sum(z_part(target)).astype(BF16)
        send(zs1.at[i], zr1.at[i], z1_ss.at[i], z1_rs.at[i], dev(0, 0, hop, 0))
    dc_group(2)
    dc_send(PLACE[2, 2], 2 - 2 * par, 2 * par)
    for o, hop in (((1, 2), (1, 0)), ((2, 1), (0, 1)), ((3, 2), (3, 0)), ((2, 3), (0, 3))):
        dc_send(PLACE[o], *hop)
    for i, target in ((2, -1), (3, 1)):
        zs2[i] = z_sum(z_part(target)).astype(BF16)
        send(zs2.at[i], zr2.at[i], z2_ss.at[i], z2_rs.at[i], dev(0, 0, target, 0))
    dc_group(1)
    for o, hop in (((1, 1), (1, 0)), ((3, 1), (0, 1)), ((3, 3), (3, 0)), ((1, 3), (0, 3))):
        dc_send(PLACE[o], *hop)
    for target in (0, -2, 2):
        zp[z_part(target)] = z_sum(z_part(target))
    dc_group(0)
    for i in range(3):
        arrived(zr1.at[i], z1_ss.at[i], z1_rs.at[i])
    far = zr1[0].astype(F32)
    down = zp[z_part(-2)] + zr1[1].astype(F32) + jnp.where(zpar == 0, far, 0.0)
    up = zp[z_part(2)] + zr1[2].astype(F32) + jnp.where(zpar == 1, far, 0.0)
    zs2[0] = down.astype(BF16)
    zs2[1] = up.astype(BF16)
    send(zs2.at[0], zr2.at[0], z2_ss.at[0], z2_rs.at[0], dev(0, 0, -2, 0))
    send(zs2.at[1], zr2.at[1], z2_ss.at[1], z2_rs.at[1], dev(0, 0, 2, 0))

    dc_wait((2, 2), (2, 1), (2, 3))
    dc_hub((2, 0), (2, 1), (2, 3))
    dc_wait((1, 2), (3, 2))
    dc_hub((0, 2), (1, 2), (3, 2))
    for o, other in (((0, 1), (1, 1)), ((1, 0), (1, 3)), ((0, 3), (3, 3)), ((3, 0), (3, 1))):
        dc_wait(other)
        dc_hub(o, other)

    total = zp[0]
    for i in (2, 3, 0, 1):
        arrived(zr2.at[i], z2_ss.at[i], z2_rs.at[i])
        total = total + zr2[i].astype(F32)
    dq_out[...] = (total * cot[0:1, :]).T
    total = dcf[0]
    for i in range(6):
        arrived(xr2.at[i], x2_ss.at[i], x2_rs.at[i])
        total = total + xr2[i].astype(F32)
    dc_out[...] = total
    for copy in pending:
        copy.wait_send()


def shards(queries, candidates, block_mask, row_class, col_class, cotangent):
    dma = pltpu.SemaphoreType.DMA
    vmem = pltpu.VMEM
    block = (D, ROWS)
    scratch = [
        vmem((NB, NB), jnp.int32),
        vmem((NB, ROWS), jnp.int32),
        vmem((NB, ROWS), jnp.int32),
        vmem((NX, ROWS), F32),
        vmem((SLOTS, SENT, D), BF16),
        vmem((SLOTS, ROWS, D), BF16),
        vmem((D, TILE), BF16),
        vmem((TILE, TILE), BF16),
        vmem((8, TILE), F32),
        vmem((8, TILE), F32),
        vmem((NB, TILE), BF16),
        vmem((TILE, NB), BF16),
        vmem((8,) + block, F32),
        vmem((8,) + block, F32),
        vmem((SLOTS, ROWS), F32),
        vmem((SLOTS, ROWS), F32),
        vmem((NZ, SLOTS, ROWS), F32),
        vmem((2, SLOTS, ROWS), F32),
        vmem((2, D, TILE), BF16),
        vmem((SLOTS, ROWS, D), F32),
        vmem((2, 4, 2 * D, ROWS), BF16),
        vmem((2, 4, 2 * D, ROWS), BF16),
        vmem((8,) + block, F32),
        vmem((3,) + block, BF16),
        vmem((3,) + block, BF16),
        vmem((4,) + block, BF16),
        vmem((4,) + block, BF16),
        vmem((9, ROWS, D), BF16),
        vmem((9, ROWS, D), BF16),
        vmem((6, ROWS, D), BF16),
        vmem((6, ROWS, D), BF16),
        dma((6,)),
        dma((7,)), dma((7,)), dma((2,)), dma((2,)),
        dma((16,)), dma((16,)), dma((8,)), dma((8,)), dma((2,)), dma((2,)),
        dma((3,)), dma((3,)), dma((4,)), dma((4,)), dma((9,)), dma((9,)), dma((6,)), dma((6,)),
    ]
    out = vmem((ROWS, D), F32)
    dq, dc = pl.pallas_call(
        kernel,
        out_shape=(out, out),
        in_specs=[pl.BlockSpec(memory_space=pl.ANY)] * 6,
        out_specs=(pl.BlockSpec(memory_space=vmem), pl.BlockSpec(memory_space=vmem)),
        scratch_shapes=scratch,
        compiler_params=pltpu.CompilerParams(
            collective_id=0, has_side_effects=True, vmem_limit_bytes=56 * 2**20
        ),
    )(
        queries,
        candidates,
        block_mask,
        row_class.reshape(NB, ROWS),
        col_class.reshape(NB, ROWS),
        cotangent.reshape(NX, ROWS),
    )
    scale = 1.0 / math.sqrt(D)
    return dq * scale, dc * scale


def solution(mesh):
    in_specs = (P(("row", "col"), None), P(("row", "col"), None), P(), P(), P(), P("row"))
    out_specs = (P(("row", "col"), None), P(("row", "col"), None))
    return jax.shard_map(shards, mesh=mesh, in_specs=in_specs, out_specs=out_specs, check_vma=False)
```

```python
import math

import jax
import jax.numpy as jnp
from jax import lax
from jax.experimental import pallas as pl
from jax.experimental.pallas import tpu as pltpu
from jax.sharding import PartitionSpec as P

MESH = pl.DeviceIdType.MESH
F32 = jnp.float32
BF16 = jnp.bfloat16
ROWS = 128
SENT = ROWS + 16
D = 256
NX, NY, NZ = 4, 4, 8
TILE = 2048
SLOTS = 16
CLASSES = 8
NB = 256
LOG2E = math.log2(math.e)
NT = (((1,), (1,)), ((), ()))
TN = (((0,), (0,)), ((), ()))

OFFSETS = [(0, 0), (1, 0), (3, 0), (2, 0), (0, 1), (0, 3), (0, 2)]
OFFSETS += [(1, 1), (1, 3), (3, 1), (3, 3), (1, 2), (3, 2), (2, 1), (2, 3), (2, 2)]
PLACE = {o: i for i, o in enumerate(OFFSETS)}
GROUPS = ((0, 7), (7, 11), (11, 16))
Q_OFFSETS = [(0, 0), (-2, 0), (2, 0), (-1, 0), (0, 1), (-2, 1), (2, 1), (-1, 1)]
Q_OFFSETS += [(1, 0), (4, 0), (-3, 0), (3, 0), (1, 1), (4, 1), (-3, 1), (3, 1)]
Q_PLACE = {o: i for i, o in enumerate(Q_OFFSETS)}
OWN_CORE = (0, 1, 2, 3, 8, 9, 10, 11)


def split2(value):
    high = value.astype(BF16)
    return high, (value - high.astype(F32)).astype(BF16)


def as_row(rows):
    return jnp.concatenate(rows, axis=1)


def lanes_of(slot):
    return slice(slot * ROWS, (slot + 1) * ROWS)


def kernel(
    q_own, c_own, mask_hbm, rc_hbm, cc_hbm, cot_hbm, dq_out, dc_out,
    mask_ref, rc_ref, cc_ref, cot_ref,
    qg, cg, qt, e, m_ref, l_ref, pt, pc, ot, post, st_own, st_sib, st_all, st_end, aqt,
    dcf, zs_sib, zr_sib, zp, zs1, zr1, zs2, zr2, xs1, xr1, xs2, xr2,
    in_s, q_ss, q_rs, qf_ss, qf_rs, c_ss, c_rs, t_ss, t_rs, zb_ss, zb_rs,
    z1_ss, z1_rs, z2_ss, z2_rs, x1_ss, x1_rs, x2_ss, x2_rs,
):
    kk = LOG2E / math.sqrt(D)
    x = lax.axis_index("col")
    row = lax.axis_index("row")
    core = row % 2
    z = (row // 2) % NZ
    y = row // (2 * NZ)
    par = (x + y) % 2
    zpar = z % 2
    zsig = 1 - 2 * zpar

    def dev(dx, dy, dz, dcore):
        ny, nz, nc = (y + dy) % NY, (z + dz) % NZ, (core + dcore) % 2
        return ((ny * NZ + nz) * 2 + nc, (x + dx) % NX)

    sibling = dev(0, 0, 0, 1)
    pending = []

    def send(src, dst, ssem, rsem, to):
        copy = pltpu.make_async_remote_copy(
            src_ref=src, dst_ref=dst, send_sem=ssem, recv_sem=rsem, device_id=to, device_id_type=MESH
        )
        copy.start()
        pending.append(copy)

    def arrived(dst, ssem, rsem):
        pltpu.make_async_remote_copy(
            src_ref=dst, dst_ref=dst, send_sem=ssem, recv_sem=rsem, device_id=sibling, device_id_type=MESH
        ).wait_recv()

    barrier = pltpu.get_barrier_semaphore()
    peers = [dev(0, 0, d, 0) for d in (2, 6, 1, 7)]
    peers += [dev(d, 0, 0, 0) for d in (2, 1, 3)]
    peers += [dev(0, d, 0, 0) for d in (2, 1, 3)]
    peers += [sibling]
    for peer in peers:
        pl.semaphore_signal(barrier, inc=1, device_id=peer, device_id_type=MESH)
    loads = [
        pltpu.make_async_copy(src, dst, in_s.at[i])
        for i, (src, dst) in enumerate(
            (
                (q_own, qg.at[0, pl.ds(0, ROWS)]), (cot_hbm, cot_ref), (c_own, cg.at[0]),
                (mask_hbm, mask_ref), (rc_hbm, rc_ref), (cc_hbm, cc_ref),
            )
        )
    ]
    for load in loads:
        load.start()
    for load in loads[:3]:
        load.wait()
    own_cot = cot_ref[pl.ds(x, 1), :]
    high = own_cot.astype(BF16).astype(F32)
    middle = (own_cot - high).astype(BF16).astype(F32)
    low = own_cot - high - middle
    part_row = lax.broadcasted_iota(jnp.int32, (16, D), 0)
    parts = jnp.where(part_row == 0, jnp.concatenate([high, middle], axis=1), 0.0)
    parts = jnp.where(part_row == 1, jnp.concatenate([low, low], axis=1), parts)
    qg[0, ROWS:SENT, :] = parts.astype(BF16)
    pl.semaphore_wait(barrier, len(peers))

    z_hops = (2, -2, 1, -1)

    def q_first(i):
        hop = z_hops[i]
        send(qg.at[0], qg.at[Q_PLACE[-hop, 0]], q_ss.at[i], q_rs.at[i], dev(0, 0, hop, 0))

    def c_first(o):
        back = PLACE[(-o[0]) % NX, (-o[1]) % NY]
        send(cg.at[0], cg.at[back], c_ss.at[back], c_rs.at[back], dev(o[0], o[1], 0, 0))

    for i in range(4):
        q_first(i)
    for o in ((2, 0), (0, 2), (1, 0), (0, 1), (3, 0), (0, 3)):
        c_first(o)
    for load in loads[3:]:
        load.wait()

    lane256 = lax.broadcasted_iota(jnp.int32, (SLOTS, NB), 1)
    slot256 = lax.broadcasted_iota(jnp.int32, (SLOTS, NB), 0)
    q_block = jnp.zeros((SLOTS, NB), jnp.int32)
    for s, (dz, dc) in enumerate(Q_OFFSETS):
        block = ((y * NZ + (z + dz) % NZ) * 2 + (core + dc) % 2) * NX + x
        q_block = jnp.where(slot256 == s, block, q_block)
    sel_q = jnp.where(lane256 == q_block, 1.0, 0.0).astype(BF16)
    c_block = jnp.zeros((SLOTS, NB), jnp.int32)
    for b, (dx, dy) in enumerate(OFFSETS):
        block = ((((y + dy) % NY) * NZ + z) * 2 + core) * NX + (x + dx) % NX
        c_block = jnp.where(slot256 == b, block, c_block)
    sel_c = jnp.where(lane256 == c_block, 1.0, 0.0).astype(BF16)
    mask = mask_ref[...].astype(F32).astype(BF16)
    rc_all = rc_ref[...].astype(F32).astype(BF16)
    cc_all = cc_ref[...].astype(F32)
    m_sel = jnp.dot(sel_q, mask, preferred_element_type=F32).astype(BF16)
    rc = jnp.dot(sel_q, rc_all, preferred_element_type=F32)
    cc = jnp.dot(sel_c, cc_all.astype(BF16), preferred_element_type=F32)
    lane128 = lax.broadcasted_iota(jnp.int32, (ROWS, ROWS), 1)
    hist = jnp.zeros((NB, ROWS), F32)
    for k in range(CLASSES):
        column = jnp.where(lane128 == k, 1.0, 0.0).astype(BF16)
        same = jnp.where(cc_all == float(k), 1.0, 0.0).astype(BF16)
        hist = hist + jnp.dot(same, column, preferred_element_type=F32)
    per_class = jnp.dot(m_sel, hist.astype(BF16), preferred_element_type=F32)
    count = jnp.zeros((SLOTS, ROWS), F32)
    for k in range(CLASSES):
        count = jnp.where(rc == float(k), per_class[:, k : k + 1], count)
    per_count = 1.0 / jnp.maximum(count, 1.0)
    class_of = (lax.broadcasted_iota(jnp.int32, (ROWS, ROWS), 0) % CLASSES).astype(F32)
    slot_of = lax.broadcasted_iota(jnp.int32, (ROWS, ROWS), 0) // CLASSES

    def repeated(value):
        return jnp.broadcast_to(value[:, None, :], (SLOTS, CLASSES, NB)).reshape(ROWS, NB)

    sel_c_rows = repeated(sel_c.astype(F32)).astype(BF16)
    m_sel_rows = repeated(m_sel.astype(F32)).astype(BF16)
    hit_q = lax.dot_general(sel_c_rows, m_sel, NT, preferred_element_type=F32)
    hit_c = lax.dot_general(m_sel_rows, sel_c, NT, preferred_element_type=F32)
    for s in range(SLOTS):
        picked = jnp.where(rc[s : s + 1, :] == class_of, hit_q[:, s : s + 1], 0.0).astype(BF16)
        pt[0:ROWS, lanes_of(s)] = picked
        pt[ROWS:NB, lanes_of(s)] = picked
        picked = jnp.where(cc[s : s + 1, :] == class_of, hit_c[:, s : s + 1], 0.0).T.astype(BF16)
        pc[lanes_of(s), 0:ROWS] = picked
        pc[lanes_of(s), ROWS:NB] = picked

    def c_here(*offsets):
        for o in offsets:
            arrived(cg.at[PLACE[o]], c_ss.at[PLACE[o]], c_rs.at[PLACE[o]])

    def c_forward(o, dx, dy):
        there = PLACE[(o[0] - dx) % NX, (o[1] - dy) % NY]
        send(cg.at[PLACE[o]], cg.at[there], c_ss.at[there], c_rs.at[there], dev(dx, dy, 0, 0))

    def q_arrived(i, dz):
        slot = Q_PLACE[dz, 0]
        arrived(qg.at[slot], q_ss.at[i], q_rs.at[i])

    def q_pass(i):
        here, there = qg.at[pl.ds(8 * i, 4)], qg.at[pl.ds(8 * i + 4, 4)]
        send(here, there, qf_ss.at[i], qf_rs.at[i], sibling)

    def q_passed(i):
        arrived(qg.at[pl.ds(8 * i + 4, 4)], qf_ss.at[i], qf_rs.at[i])

    q_far = Q_PLACE[-2, 0] + zpar * (Q_PLACE[2, 0] - Q_PLACE[-2, 0])
    onward = (
        (4, q_far, Q_PLACE[4, 0], 2 * zsig),
        (5, Q_PLACE[-2, 0], Q_PLACE[-3, 0], 1),
        (6, Q_PLACE[2, 0], Q_PLACE[3, 0], -1),
    )

    c_here((2, 0), (0, 2))
    for hop in (1, 3):
        c_forward((2, 0), 0, hop)
        c_forward((0, 2), hop, 0)
    q_arrived(0, -2)
    q_arrived(1, 2)
    for i, here, there, dz in onward:
        send(qg.at[here], qg.at[there], q_ss.at[i], q_rs.at[i], dev(0, 0, dz, 0))
    far = PLACE[2, 0] + par * (PLACE[0, 2] - PLACE[2, 0])
    there = PLACE[2, 2]
    send(cg.at[far], cg.at[there], c_ss.at[there], c_rs.at[there], dev(2 * par, 2 - 2 * par, 0, 0))
    for o, dx, dy in (((0, 1), 3, 0), ((0, 3), 1, 0), ((1, 0), 0, 1), ((3, 0), 0, 3)):
        c_here(o)
        c_forward(o, dx, dy)
    q_arrived(2, -1)
    q_pass(0)

    def wave(g, q_first, q_last):
        first, last = GROUPS[g]
        rows = slice(first * ROWS, last * ROWS)
        lanes = slice(q_first * ROWS, q_last * ROWS)
        c_rows = cg[first:last].reshape((last - first) * ROWS, D)
        q_rows = qg[q_first:q_last, 0:ROWS, :].reshape((q_last - q_first) * ROWS, D)
        scores = lax.dot_general(c_rows, q_rows, NT, preferred_element_type=F32)
        top = jnp.max(scores, axis=0, keepdims=True)
        grown = jnp.exp2((scores - top) * kk)
        m_ref[g : g + 1, lanes] = top * kk
        l_ref[g : g + 1, lanes] = jnp.sum(grown, axis=0, keepdims=True)
        e[rows, lanes] = grown.astype(BF16)

    def c_wait(g):
        for slot in range(*GROUPS[g]):
            arrived(cg.at[slot], c_ss.at[slot], c_rs.at[slot])

    wave(0, 0, 4)
    q_passed(0)
    wave(0, 4, 8)
    c_wait(1)
    wave(1, 0, 8)
    for i, dz in ((3, 1), (5, -3), (6, 3), (4, 4)):
        q_arrived(i, dz)
    q_pass(1)
    wave(0, 8, 12)
    wave(1, 8, 12)
    c_wait(2)
    wave(2, 0, 12)
    q_passed(1)
    for g in range(3):
        wave(g, 12, 16)
    tops = m_ref[0:3, :]
    top_tile = jnp.max(tops, axis=0, keepdims=True)
    mass = jnp.sum(l_ref[0:3, :] * jnp.exp2(tops - top_tile), axis=0, keepdims=True)
    log_tile = top_tile + jnp.log2(mass)

    places = [2 * ((z + dz) % NZ) + (core + dc) % 2 for dz, dc in Q_OFFSETS]

    def slot_rows(ref):
        return as_row([ref[pl.ds(place, 1), :] for place in places])

    for s, place in enumerate(places):
        st_own[pl.ds(place, 1), :] = log_tile[:, lanes_of(s)]
    send(st_own, st_sib, t_ss.at[0], t_rs.at[0], sibling)
    for s in range(SLOTS):
        qt[:, lanes_of(s)] = qg[s, 0:ROWS, :].T
    arrived(st_sib, t_ss.at[0], t_rs.at[0])
    log_a, log_b = st_own[...], st_sib[...]
    top = jnp.maximum(log_a, log_b)
    st_all[z] = top + jnp.log2(jnp.exp2(log_a - top) + jnp.exp2(log_b - top))
    for d in (4, 3, 5, 2, 6, 1, 7):
        send(st_all.at[z], st_all.at[z], t_ss.at[d], t_rs.at[d], dev(0, 0, d, 0))

    log_pair = slot_rows(st_all.at[z])
    shrink = jnp.exp2(tops - log_pair)
    own_class = [
        jnp.where((cc[b : b + 1, :] == class_of) & (slot_of == b), 1.0, 0.0).astype(BF16) for b in range(SLOTS)
    ]
    sums = jnp.dot(
        jnp.concatenate(own_class, axis=1), cg[...].reshape(TILE, D), preferred_element_type=F32
    )
    sums = jnp.concatenate(split2(sums), axis=0)

    def c_times_e(first):
        lanes = slice(first * ROWS, (first + 4) * ROWS)
        total = None
        for g, (start, stop) in enumerate(GROUPS):
            c_rows = cg[start:stop].reshape((stop - start) * ROWS, D)
            part = lax.dot_general(
                c_rows, e[start * ROWS : stop * ROWS, lanes], TN, preferred_element_type=F32
            )
            part = part * shrink[g : g + 1, lanes]
            total = part if total is None else total + part
        hits = lax.dot_general(sums, pt[:, lanes], TN, preferred_element_type=F32)
        return total, hits

    for half, first in enumerate((4, 12)):
        total, hits = c_times_e(first)
        for s in range(4):
            zs_sib[half, s, 0:D, :] = total[:, lanes_of(s)].astype(BF16)
            zs_sib[half, s, D : 2 * D, :] = hits[:, lanes_of(s)].astype(BF16)
        send(zs_sib.at[half], zr_sib.at[half], zb_ss.at[half], zb_rs.at[half], sibling)
    for half, first in enumerate((0, 8)):
        total, hits = c_times_e(first)
        for s in range(4):
            ot[4 * half + s] = total[:, lanes_of(s)]
            post[4 * half + s] = hits[:, lanes_of(s)]

    cot = []
    for s in range(SLOTS):
        parts = qg[s, ROWS:SENT, :].astype(F32)
        cot.append(parts[0:1, 0:ROWS] + parts[0:1, ROWS:D] + parts[1:2, 0:ROWS])
    cot = jnp.concatenate(cot, axis=0)
    coef_pos = cot * per_count
    weights = [
        jnp.where((rc[s : s + 1, :] == class_of) & (slot_of == s), -coef_pos[s : s + 1, :], 0.0)
        for s in range(SLOTS)
    ]
    weights = jnp.concatenate(split2(jnp.concatenate(weights, axis=1)), axis=0)
    sums_q = jnp.dot(weights, qg[:, 0:ROWS, :].reshape(TILE, D), preferred_element_type=F32)
    sums_q = sums_q[0:ROWS, :] + sums_q[ROWS:NB, :]
    sums_q = jnp.concatenate(split2(sums_q), axis=0)
    soft_row = as_row([(count * per_count)[s : s + 1, :] for s in range(SLOTS)])
    cot_row = as_row([cot[s : s + 1, :] for s in range(SLOTS)])

    for d in (1, 7, 2, 6, 3, 5, 4):
        slot = (z - d + NZ) % NZ
        arrived(st_all.at[slot], t_ss.at[d], t_rs.at[d])
    top = st_all[0]
    for s in range(1, NZ):
        top = jnp.maximum(top, st_all[s])
    mass = jnp.zeros((SLOTS, ROWS), F32)
    for s in range(NZ):
        mass = mass + jnp.exp2(st_all[s] - top)
    st_end[0] = top
    st_end[1] = 1.0 / mass
    top_row = slot_rows(st_end.at[0])
    soft_row = soft_row * slot_rows(st_end.at[1])
    a_groups = soft_row * cot_row * jnp.exp2(tops - top_row)
    a_pair = soft_row * jnp.exp2(log_pair - top_row)

    def z_part(dz):
        return OWN_CORE.index(Q_PLACE[dz, 0])

    def z_sum(i):
        s = OWN_CORE[i]
        half, j = i // 4, i % 4
        soft = ot[i] + zr_sib[half, j, 0:D, :].astype(F32)
        hits = post[i] + zr_sib[half, j, D : 2 * D, :].astype(F32)
        return soft * a_pair[:, lanes_of(s)] - hits * per_count[s : s + 1, :]

    for half in range(2):
        arrived(zr_sib.at[half], zb_ss.at[half], zb_rs.at[half])

    def dc_group(g):
        first, last = GROUPS[g]
        rows = slice(first * ROWS, last * ROWS)
        aqt[g % 2] = (qt[...].astype(F32) * a_groups[g : g + 1, :]).astype(BF16)
        part = lax.dot_general(e[rows, :], aqt[g % 2], NT, preferred_element_type=F32)
        part = part + jnp.dot(pc[rows, :], sums_q, preferred_element_type=F32)
        dcf[first:last] = part.reshape(last - first, ROWS, D)

    def dc_send(slot, dx, dy):
        i = slot - 7
        xs1[i] = dcf[slot].astype(BF16)
        send(xs1.at[i], xr1.at[i], x1_ss.at[i], x1_rs.at[i], dev(dx, dy, 0, 0))

    def dc_hub(o, *others):
        total = dcf[PLACE[o]]
        for other in others:
            total = total + xr1[PLACE[other] - 7].astype(F32)
        if o in ((2, 0), (0, 2)):
            total = total + jnp.where(par == o[0] // 2, xr1[PLACE[2, 2] - 7].astype(F32), 0.0)
        i = PLACE[o] - 1
        xs2[i] = total.astype(BF16)
        send(xs2.at[i], xr2.at[i], x2_ss.at[i], x2_rs.at[i], dev(o[0], o[1], 0, 0))

    def dc_wait(*slots):
        for o in slots:
            i = PLACE[o] - 7
            arrived(xr1.at[i], x1_ss.at[i], x1_rs.at[i])

    for i, (target, hop) in enumerate(((4, -2 * zsig), (-3, -1), (3, 1))):
        zs1[i] = z_sum(z_part(target)).astype(BF16)
        send(zs1.at[i], zr1.at[i], z1_ss.at[i], z1_rs.at[i], dev(0, 0, hop, 0))
    dc_group(2)
    dc_send(PLACE[2, 2], 2 - 2 * par, 2 * par)
    for o, hop in (((1, 2), (1, 0)), ((2, 1), (0, 1)), ((3, 2), (3, 0)), ((2, 3), (0, 3))):
        dc_send(PLACE[o], *hop)
    for i, target in ((2, -1), (3, 1)):
        zs2[i] = z_sum(z_part(target)).astype(BF16)
        send(zs2.at[i], zr2.at[i], z2_ss.at[i], z2_rs.at[i], dev(0, 0, target, 0))
    dc_group(1)
    for o, hop in (((1, 1), (1, 0)), ((3, 1), (0, 1)), ((3, 3), (3, 0)), ((1, 3), (0, 3))):
        dc_send(PLACE[o], *hop)
    for target in (0, -2, 2):
        zp[z_part(target)] = z_sum(z_part(target))
    dc_group(0)
    for i in range(3):
        arrived(zr1.at[i], z1_ss.at[i], z1_rs.at[i])
    far = zr1[0].astype(F32)
    down = zp[z_part(-2)] + zr1[1].astype(F32) + jnp.where(zpar == 0, far, 0.0)
    up = zp[z_part(2)] + zr1[2].astype(F32) + jnp.where(zpar == 1, far, 0.0)
    zs2[0] = down.astype(BF16)
    zs2[1] = up.astype(BF16)
    send(zs2.at[0], zr2.at[0], z2_ss.at[0], z2_rs.at[0], dev(0, 0, -2, 0))
    send(zs2.at[1], zr2.at[1], z2_ss.at[1], z2_rs.at[1], dev(0, 0, 2, 0))

    dc_wait((2, 2), (2, 1), (2, 3))
    dc_hub((2, 0), (2, 1), (2, 3))
    dc_wait((1, 2), (3, 2))
    dc_hub((0, 2), (1, 2), (3, 2))
    for o, other in (((0, 1), (1, 1)), ((1, 0), (1, 3)), ((0, 3), (3, 3)), ((3, 0), (3, 1))):
        dc_wait(other)
        dc_hub(o, other)

    total = zp[0]
    for i in (2, 3, 0, 1):
        arrived(zr2.at[i], z2_ss.at[i], z2_rs.at[i])
        total = total + zr2[i].astype(F32)
    dq_out[...] = (total * cot[0:1, :]).T
    total = dcf[0]
    for i in range(6):
        arrived(xr2.at[i], x2_ss.at[i], x2_rs.at[i])
        total = total + xr2[i].astype(F32)
    dc_out[...] = total
    for copy in pending:
        copy.wait_send()


def shards(queries, candidates, block_mask, row_class, col_class, cotangent):
    dma = pltpu.SemaphoreType.DMA
    vmem = pltpu.VMEM
    block = (D, ROWS)
    scratch = [
        vmem((NB, NB), jnp.int32),
        vmem((NB, ROWS), jnp.int32),
        vmem((NB, ROWS), jnp.int32),
        vmem((NX, ROWS), F32),
        vmem((SLOTS, SENT, D), BF16),
        vmem((SLOTS, ROWS, D), BF16),
        vmem((D, TILE), BF16),
        vmem((TILE, TILE), BF16),
        vmem((8, TILE), F32),
        vmem((8, TILE), F32),
        vmem((NB, TILE), BF16),
        vmem((TILE, NB), BF16),
        vmem((8,) + block, F32),
        vmem((8,) + block, F32),
        vmem((SLOTS, ROWS), F32),
        vmem((SLOTS, ROWS), F32),
        vmem((NZ, SLOTS, ROWS), F32),
        vmem((2, SLOTS, ROWS), F32),
        vmem((2, D, TILE), BF16),
        vmem((SLOTS, ROWS, D), F32),
        vmem((2, 4, 2 * D, ROWS), BF16),
        vmem((2, 4, 2 * D, ROWS), BF16),
        vmem((8,) + block, F32),
        vmem((3,) + block, BF16),
        vmem((3,) + block, BF16),
        vmem((4,) + block, BF16),
        vmem((4,) + block, BF16),
        vmem((9, ROWS, D), BF16),
        vmem((9, ROWS, D), BF16),
        vmem((6, ROWS, D), BF16),
        vmem((6, ROWS, D), BF16),
        dma((6,)),
        dma((7,)), dma((7,)), dma((2,)), dma((2,)),
        dma((16,)), dma((16,)), dma((8,)), dma((8,)), dma((2,)), dma((2,)),
        dma((3,)), dma((3,)), dma((4,)), dma((4,)), dma((9,)), dma((9,)), dma((6,)), dma((6,)),
    ]
    out = vmem((ROWS, D), F32)
    dq, dc = pl.pallas_call(
        kernel,
        out_shape=(out, out),
        in_specs=[pl.BlockSpec(memory_space=pl.ANY)] * 6,
        out_specs=(pl.BlockSpec(memory_space=vmem), pl.BlockSpec(memory_space=vmem)),
        scratch_shapes=scratch,
        compiler_params=pltpu.CompilerParams(
            collective_id=0, has_side_effects=True, vmem_limit_bytes=56 * 2**20
        ),
    )(
        queries,
        candidates,
        block_mask,
        row_class.reshape(NB, ROWS),
        col_class.reshape(NB, ROWS),
        cotangent.reshape(NX, ROWS),
    )
    scale = 1.0 / math.sqrt(D)
    return dq * scale, dc * scale


def solution(mesh):
    in_specs = (P(("row", "col"), None), P(("row", "col"), None), P(), P(), P(), P("row"))
    out_specs = (P(("row", "col"), None), P(("row", "col"), None))
    return jax.shard_map(shards, mesh=mesh, in_specs=in_specs, out_specs=out_specs, check_vma=False)
```
